512 devices in a mesh: frames: 4 (over y_hi, core), tiles: 128 (over z, y_lo, x).
Axes of the slice: x: 4, y: 8 (y_hi: 2, y_lo: 4; y = y_hi * 4 + y_lo), z: 8, core: 2. Of those that a mesh axis runs over, the one named last changes fastest.
Arguments:
- frames: float32 [80, 8192, 320], P('frames', 'tiles'), may hold values from -6 to 6
- live_first: int32 [128], P('tiles'), may hold values from 0 to 3, as said below
- live_count: int32 [128], P('tiles'), may hold values from 1 to 4, as said below
- shifts: int32 [2, 2], replicated, may hold values from 1 to 63, as said below
Outputs:
- restored_image: float32 [8192, 320], P('tiles')
The draws below stay inside these ranges and needn't reach their ends.
Inputs may be any that keep to these rules, and one draw needn't show every extreme that they name: live_first[a] + live_count[a] <= 4 for every tile a. `live_count`: each tile has at least one live subfield column. shifts[0] = (1, q) and shifts[1] = (p, 1) with q and p between 1 and 63, one of q and p equal to 63.
All inputs are finite; a program needn't handle non-finite values.
Results may differ from the reference program's by a relative error of at most 0.0003.
Values sent between devices are 32-bit elements; how exact they have to be, the bound alone decides.
No kernel may reach another device: no remote copies, remote signals or barrier semaphores. Data moves between devices by JAX's collectives and lax.ppermute only.
A program may use at most 64 MiB of HBM per device.

```python
import jax
import jax.numpy as jnp
from jax import lax

S = 128
TH = 64
NB = 4
COLS = 320
NSHIFT = 2
FRAMES = 80
TILES = 128
NY = 8192


def live_runs(key):
    tile_ids = jnp.arange(TILES, dtype=jnp.int32)
    counts = jax.random.randint(jax.random.fold_in(key, 11), (TILES,), 1, NB + 1)
    counts = jnp.where(tile_ids == 0, 1, counts)
    counts = jnp.where(tile_ids == TILES // 2, NB, counts)
    starts = jax.random.randint(jax.random.fold_in(key, 12), (TILES,), 0, 65536)
    starts = starts % (NB - counts + 1)
    starts = jnp.where(tile_ids == 0, NB - 1, starts)
    return (starts.astype(jnp.int32), counts.astype(jnp.int32))


def draw_live_first(key, part):
    starts, counts = live_runs(key)
    return starts


def draw_live_count(key, part):
    starts, counts = live_runs(key)
    return counts


def draw_shifts(key, part):
    key = jax.random.fold_in(key, 3)
    offsets = jax.random.randint(key, (2,), 1, S // 2)
    flag = jax.random.randint(jax.random.fold_in(key, 7), (), 0, 2)
    top_value = offsets[0] * 0 + (S // 2 - 1)
    column_off = jnp.where(flag == 1, top_value, offsets[0])
    row_off = jnp.where(flag == 1, offsets[1], top_value)
    first_pair = jnp.stack([offsets[0] * 0 + 1, column_off])
    second_pair = jnp.stack([row_off, offsets[1] * 0 + 1])
    return jnp.stack([first_pair, second_pair]).astype(jnp.int32)


def shard_levels(rng, shape, split, least, largest):
    def one(axis_at, shards_of):
        steps = jax.random.uniform(jax.random.fold_in(jax.random.fold_in(rng, 6), axis_at), (shards_of,), jnp.float32, least / len(split), largest / len(split))
        return jnp.repeat(jnp.exp(steps), shape[axis_at] // shards_of).reshape((-1,) + (1,) * (len(shape) - axis_at - 1))

    factor_of = one(*split[0])
    for cut in split[1:]:
        factor_of = factor_of * one(*cut)
    return factor_of


def bell_draw(stream_key, extent, width, limit, shards=(), held_as=jnp.bfloat16):
    drawn = jax.random.normal(stream_key, extent, jnp.float32) * width
    if len(shards) > 0:
        drawn = shard_levels(stream_key, extent, shards, -0.22, 0.18) * drawn
    return jnp.clip(drawn, min=-limit, max=limit).astype(held_as)


def setup_inputs(seed: int = 0) -> dict:
    arg_keys = jax.random.split(jax.random.key(seed), 5)
    return {
        "frames": bell_draw(arg_keys[0], (FRAMES, NY, COLS), 1.0, 6.0, ((0, 4), (1, 128)), jnp.float32),
        "live_first": draw_live_first(jax.random.fold_in(arg_keys[4], 71), 0),
        "live_count": draw_live_count(jax.random.fold_in(arg_keys[4], 71), 0),
        "shifts": draw_shifts(jax.random.fold_in(arg_keys[4], 71), 0),
    }


ridge_term = 0.1
share_term = 0.0001
tiny_term = 1e-06

def taper(side_len):
    position = jnp.arange(side_len, dtype=jnp.float32)
    single = jnp.sin(jnp.pi * (position + 0.5) / side_len) ** 2
    return single[:, None] * single[None, :]

def spectral_eigen(shifts, side_len):
    frequency = jnp.arange(side_len, dtype=jnp.int32)
    eigen_total = jnp.full((side_len, side_len), ridge_term, jnp.float32)
    for s in range(shifts.shape[0]):
        phase_angle = (frequency[:, None] * shifts[s, 0] + frequency[None, :] * shifts[s, 1]) % side_len
        eigen_total = eigen_total + 2.0 - 2.0 * jnp.cos(2.0 * jnp.pi * phase_angle.astype(jnp.float32) / side_len)
    return eigen_total

def solve_tile(power_sum, cross_list, shifts, eigen, window):
    mean_power = lax.optimization_barrier(jnp.mean(power_sum, axis=(1, 2), keepdims=True))
    normal_rhs = jnp.zeros_like(power_sum)
    for s in range(shifts.shape[0]):
        row_step = shifts[s, 0]
        col_step = shifts[s, 1]
        partner = jnp.roll(power_sum, (-row_step, -col_step), axis=(1, 2))
        scale_term = jnp.sqrt(power_sum * partner + share_term * mean_power * mean_power) + tiny_term
        sine_diff = cross_list[s] / scale_term
        normal_rhs = normal_rhs + sine_diff - jnp.roll(sine_diff, (row_step, col_step), axis=(1, 2))
    phase_map = jnp.real(jnp.fft.ifft2(jnp.fft.fft2(normal_rhs) / eigen))
    amplitude = jnp.sqrt(power_sum)
    rebuilt = jnp.real(jnp.fft.ifft2(amplitude * jnp.cos(phase_map) + 1j * (amplitude * jnp.sin(phase_map))))
    return rebuilt * window

def reference(frames, live_first, live_count, shifts):
    side_len = S
    half_side = TH
    window = taper(side_len)
    eigen = spectral_eigen(shifts, side_len)
    padded = jnp.concatenate([frames, jnp.zeros((FRAMES, half_side, COLS), frames.dtype)], axis=1)
    column_ids = jnp.arange(NB, dtype=jnp.int32)

    def one_tile(tile_index):
        stacked = lax.dynamic_slice_in_dim(padded, tile_index * half_side, side_len, 1)
        patches = jnp.stack([stacked[:, :, c * half_side:c * half_side + side_len] for c in range(NB)], axis=1)
        spectra = jnp.fft.fft2(patches * window)
        power_sum = lax.optimization_barrier(jnp.mean(jnp.real(spectra) ** 2 + jnp.imag(spectra) ** 2, axis=0))
        cross_list = []
        for s in range(NSHIFT):
            partner = jnp.roll(spectra, (-shifts[s, 0], -shifts[s, 1]), axis=(2, 3))
            cross_list.append(lax.optimization_barrier(jnp.mean(jnp.imag(spectra * jnp.conj(partner)), axis=0)))
        rebuilt = solve_tile(power_sum, cross_list, shifts, eigen, window)
        live_mask = (column_ids >= live_first[tile_index]) & (column_ids < live_first[tile_index] + live_count[tile_index])
        rebuilt = rebuilt * live_mask[:, None, None].astype(rebuilt.dtype)
        padding = jnp.zeros((1, side_len, half_side), rebuilt.dtype)
        halves = jnp.concatenate([rebuilt[:, :, :half_side], padding], axis=0) + jnp.concatenate([padding, rebuilt[:, :, half_side:]], axis=0)
        return jnp.transpose(halves, (1, 0, 2)).reshape(side_len, COLS)
    blocks = lax.map(one_tile, jnp.arange(TILES, dtype=jnp.int32))
    upper_rows = blocks[:, :half_side]
    lower_rows = blocks[:, half_side:]
    moved = jnp.concatenate([jnp.zeros_like(lower_rows[:1]), lower_rows[:-1]], axis=0)
    return (upper_rows + moved).reshape(NY, COLS)
```

```python
import functools

import jax
import jax.numpy as jnp
import ml_dtypes
import numpy as np
from jax import lax
from jax.experimental import pallas as pl
from jax.experimental.pallas import tpu as pltpu
from jax.sharding import PartitionSpec as P

ridge_term = 0.1
share_term = 0.0001
tiny_term = 1e-06

side = 128
half = 64
width = 320
pair_width = 2 * width
folded_rows = 200
total_frames = 80
float32 = jnp.float32
bfloat16 = jnp.bfloat16
vmem_limit = 48 * 1024 * 1024


def as_pieces(table):
    upper = table.astype(np.float32).astype(ml_dtypes.bfloat16)
    lower = (table - upper.astype(np.float64)).astype(np.float32).astype(ml_dtypes.bfloat16)
    return upper, lower


def complex_tables():
    index = np.arange(side)
    angle = 2.0 * np.pi * (index[:, None] * index[None, :] % side) / side
    cosine, sine = np.cos(angle), np.sin(angle)
    taper = np.sin(np.pi * (index + 0.5) / side) ** 2
    wc, ws = taper[:, None] * cosine, taper[:, None] * sine
    right_taper = np.block([[wc, -ws], [ws, wc]])
    left_taper = np.block([[wc.T, ws.T], [-ws.T, wc.T]])
    right = np.block([[cosine, -sine], [sine, cosine]])
    left = np.block([[cosine, sine], [-sine, cosine]])
    right_back = np.block([[cosine, sine], [-sine, cosine]])
    left_back = np.block([[cosine, -sine], [sine, cosine]])
    stacked = [as_pieces(t) for t in (right_taper, left_taper, right, left, right_back, left_back)]
    flip = np.zeros((side, side), ml_dtypes.bfloat16)
    flip[index, (-index) % side] = 1
    window = (taper[:, None] * taper[None, :] / side**2).astype(np.float32)
    return np.stack([np.stack(s) for s in stacked]), flip, window


def pieces(values):
    upper = values.astype(bfloat16)
    lower = (values - upper.astype(float32)).astype(bfloat16)
    return upper, lower


def product(a, b):
    return jnp.dot(a, b, preferred_element_type=float32)


def times_table(values, table_ref):
    upper, lower = pieces(values)
    high, low = table_ref[0], table_ref[1]
    return product(upper, high) + product(lower, high) + product(upper, low)


def table_times(table_ref, values):
    upper, lower = pieces(values)
    high, low = table_ref[0], table_ref[1]
    return product(high, upper) + product(high, lower) + product(low, upper)


def upright(g):
    return jnp.concatenate([g[:, :side], g[:, side:]], axis=0)


def moved(values, row_step, col_step):
    return pltpu.roll(pltpu.roll(values, side - col_step, 1), side - row_step, 0)


def moved_back(values, row_step, col_step):
    return pltpu.roll(pltpu.roll(values, col_step, 1), row_step, 0)


def mirrored(planes, flip_ref):
    flip = flip_ref[...]
    twice_down = jnp.concatenate([flip, flip], axis=0)
    twice_across = jnp.concatenate([flip, flip], axis=1)
    tall = jnp.concatenate(planes, axis=0)
    upper, lower = pieces(tall)
    tall = product(jnp.concatenate([upper, lower], axis=1), twice_down)
    wide = jnp.concatenate([tall[i * side : (i + 1) * side] for i in range(len(planes))], axis=1)
    upper, lower = pieces(wide)
    wide = product(twice_across, jnp.concatenate([upper, lower], axis=0))
    return [wide[:, i * side : (i + 1) * side] for i in range(len(planes))]


def pack_kernel(frames_ref, *out_refs):
    base = 0
    for out_ref in out_refs:
        count = out_ref.shape[0]

        def body(i, carry, base=base, out_ref=out_ref):
            f = 2 * (base + i)
            out_ref[i] = jnp.concatenate([frames_ref[f], frames_ref[f + 1]], axis=1)
            return carry

        lax.fori_loop(0, count, body, 0)
        base += count


def add_pair(upper, lower, row_step, col_step, right_ref, left_ref, out_ref, which):
    plane = jnp.concatenate([upper, lower], axis=0)
    shifted = plane[:, half : half + 512]
    first = [plane[:, 0:128], shifted[:, 0:128], plane[:, 128:256], shifted[:, 128:256]]
    second = [shifted[:, 256:384], plane[:, 384:512], shifted[:, 384:512], plane[:, 512:640]]
    stacked = jnp.concatenate([jnp.concatenate([a, b], axis=1) for a, b in zip(first, second)], axis=0)
    g = times_table(stacked, right_ref)
    for two in range(2):
        parts = [upright(g[(2 * two + j) * side : (2 * two + j + 1) * side]) for j in range(2)]
        z = table_times(left_ref, jnp.concatenate(parts, axis=1))
        for j in range(2):
            c = 2 * two + j
            zr = z[:side, j * side : (j + 1) * side]
            zi = z[side:, j * side : (j + 1) * side]
            out_ref[which, c, 0] += zr * zr + zi * zi
            out_ref[which, c, 1] += zi * moved(zr, 1, col_step) - zr * moved(zi, 1, col_step)
            out_ref[which, c, 2] += zi * moved(zr, row_step, 1) - zr * moved(zi, row_step, 1)


def add_chunk(scalars, own_l, halo_l, own_r, halo_r, right_ref, left_ref, acc):
    row_step, col_step = scalars[0], scalars[1]

    def body(i, carry):
        add_pair(own_l[i], halo_l[i], row_step, col_step, right_ref, left_ref, acc, 0)
        add_pair(halo_r[i], own_r[i], row_step, col_step, right_ref, left_ref, acc, 1)
        return carry

    lax.fori_loop(0, own_l.shape[0], body, 0)


def start_kernel(scalars, own_r0, own_r1, right_ref, left_ref, out_ref):
    out_ref[...] = jnp.zeros_like(out_ref)

    @pl.when(scalars[3] == 1)
    def last_tile():
        blank = jnp.zeros((half, pair_width), float32)
        for own in (own_r0, own_r1):

            def body(i, carry, own=own):
                add_pair(own[i], blank, scalars[0], scalars[1], right_ref, left_ref, out_ref, 0)
                return carry

            lax.fori_loop(0, own.shape[0], body, 0)


def middle_kernel(scalars, own_l, halo_l, own_r, halo_r, right_ref, left_ref, before, out_ref):
    out_ref[...] = before[...]
    add_chunk(scalars, own_l, halo_l, own_r, halo_r, right_ref, left_ref, out_ref)


def last_kernel(scalars, own_l, halo_l, own_r, halo_r, right_ref, left_ref, before, kept, sent, acc):
    acc[...] = before[...]
    add_chunk(scalars, own_l, halo_l, own_r, halo_r, right_ref, left_ref, acc)
    lower_core = scalars[2] == 0
    for which in range(2):
        for j in range(2):
            for k in range(3):
                one, two = acc[which, j, k], acc[which, 2 + j, k]
                kept[which, j, k] = jnp.where(lower_core, one, two)
                sent[which, j, k] = jnp.where(lower_core, two, one)


def fold_kernel(scalars, kept, got, flip_ref, here_ref, there_ref):
    row_step, col_step = scalars[0], scalars[1]
    lanes = lax.broadcasted_iota(jnp.int32, (half, side), 1)
    for which, out_ref in enumerate((here_ref, there_ref)):
        planes = [kept[which, j, k] + got[which, j, k] for j in range(2) for k in range(3)]
        mirror = mirrored(planes, flip_ref)
        for j in range(2):
            power, cross_a, cross_b = planes[3 * j : 3 * j + 3]
            flip_power, flip_a, flip_b = mirror[3 * j : 3 * j + 3]
            cross_a = cross_a + moved(flip_a, 1, col_step)
            cross_b = cross_b + moved(flip_b, row_step, 1)
            out_ref[j, 0:half] = cross_a[:half]
            out_ref[j, half:side] = jnp.where(lanes < half, cross_b[:half], pltpu.roll(cross_b[half:], half, 1))
            out_ref[j, side:folded_rows] = (power + flip_power)[: folded_rows - side]


def solve_kernel(
    scalars, factors, here, there, flip_ref, right, left, right_back, left_back, inverse_eigen, window, upper_ref, lower_ref
):
    row_step, col_step = scalars[0], scalars[1]
    lanes = lax.broadcasted_iota(jnp.int32, (side, side), 1)
    blank = jnp.zeros((half, side), float32)
    planes = []
    for j in range(2):
        both = here[j] + there[j]
        crowded = both[half:side]
        planes.append(jnp.concatenate([both[side:], blank[: 2 * side - folded_rows]], axis=0))
        planes.append(jnp.concatenate([both[:half], blank], axis=0))
        spread = jnp.concatenate([crowded, pltpu.roll(crowded, half, 1)], axis=0)
        planes.append(jnp.where(lanes < half, spread, 0.0))
    mirror = mirrored(planes, flip_ref)
    scale = 0.5 / total_frames
    targets, amplitudes = [], []
    for j in range(2):
        power = jnp.concatenate([planes[3 * j][: folded_rows - side], mirror[3 * j][folded_rows - side :]], axis=0)
        power = power * scale
        cross_a = (planes[3 * j + 1] + moved(mirror[3 * j + 1], 1, col_step)) * scale
        cross_b = (planes[3 * j + 2] + moved(mirror[3 * j + 2], row_step, 1)) * scale
        level = jnp.sum(jnp.sum(power, axis=0, keepdims=True), axis=1, keepdims=True) * (1.0 / (side * side))
        floor = share_term * level * level
        target = jnp.zeros((side, side), float32)
        for cross, rows, cols in ((cross_a, 1, col_step), (cross_b, row_step, 1)):
            partner = moved(power, rows, cols)
            coherence = cross / (jnp.sqrt(power * partner + floor) + tiny_term)
            target = target + coherence - moved_back(coherence, rows, cols)
        targets.append(target)
        amplitudes.append(jnp.sqrt(power))
    z = table_times(left, upright(times_table(jnp.concatenate(targets, axis=1), right)))
    zr = z[:side] * inverse_eigen[...]
    zi = z[side:] * inverse_eigen[...]
    phase = table_times(left_back, upright(times_table(jnp.concatenate([zr, zi], axis=1), right_back)))
    cosine, sine = jnp.cos(phase), jnp.sin(phase)
    first, second = amplitudes
    wr = first * cosine[:side] - second * sine[side:]
    wi = first * sine[:side] + second * cosine[side:]
    rebuilt = table_times(left_back, upright(times_table(jnp.concatenate([wr, wi], axis=1), right_back)))
    first = rebuilt[:side] * (window[...] * factors[0])
    second = pltpu.roll(rebuilt[side:] * (window[...] * factors[1]), half, 1)
    left_part = first + jnp.where(lanes >= half, second, 0.0)
    right_part = jnp.where(lanes < half, second, 0.0)
    block = jnp.concatenate([left_part, right_part], axis=1)
    upper_ref[...] = block[:half]
    lower_ref[...] = block[half:]


def join_kernel(scalars, upper_own, upper_other, lower_own, lower_other, out_ref):
    own = upper_own[...] + lower_own[...]
    other = upper_other[...] + lower_other[...]
    lower_core = scalars[2] == 0
    left = jnp.where(lower_core, own, other)
    right = jnp.where(lower_core, other, own)
    out_ref[:, 0:128] = left[:, :128]
    out_ref[:, 128:256] = left[:, 128:] + right[:, :128]
    out_ref[:, 256:320] = right[:, 128:192]


def inverse_eigen_of(shifts):
    frequency = jnp.arange(side, dtype=jnp.int32)
    total = jnp.full((side, side), ridge_term, float32)
    for s in range(shifts.shape[0]):
        angle = (frequency[:, None] * shifts[s, 0] + frequency[None, :] * shifts[s, 1]) % side
        total = total + 2.0 - 2.0 * jnp.cos(2.0 * jnp.pi * angle.astype(float32) / side)
    return 1.0 / (total * (side * side))


smem = pl.BlockSpec(memory_space=pltpu.SMEM)
vmem = pl.BlockSpec(memory_space=pltpu.VMEM)


def call(kernel, shapes, scalar_count, array_count, scratch=(), flops=0, moved_bytes=0):
    return pl.pallas_call(
        kernel,
        out_shape=[jax.ShapeDtypeStruct(s, float32) for s in shapes],
        in_specs=[smem] * scalar_count + [vmem] * array_count,
        out_specs=[vmem] * len(shapes),
        scratch_shapes=list(scratch),
        compiler_params=pltpu.CompilerParams(vmem_limit_bytes=vmem_limit),
        cost_estimate=pl.CostEstimate(flops=flops, bytes_accessed=moved_bytes, transcendentals=0),
    )


def on_device(frames, live_first, live_count, shifts):
    pairs = frames.shape[0] // 2
    tiles = lax.axis_size("tiles")
    tile = lax.axis_index("tiles")
    core = lax.axis_index("frames") % 2
    tables, flip, window = complex_tables()
    right_taper, left_taper, right, left, right_back, left_back = [jnp.asarray(t) for t in tables]
    flip, window = jnp.asarray(flip), jnp.asarray(window)
    scalars = jnp.stack([shifts[1, 0], shifts[0, 1], core.astype(jnp.int32), (tile == tiles - 1).astype(jnp.int32)])
    columns = 2 * core + jnp.arange(2, dtype=jnp.int32)
    live = (columns >= live_first[0]) & (columns < live_first[0] + live_count[0])
    factors = live.astype(float32)

    each = pairs // 2
    tail = 1
    body = each - tail
    own_l0, own_l1, own_r0, own_r1 = call(
        pack_kernel, [(n, half, pair_width) for n in (body, tail, body, tail)], 0, 1, moved_bytes=4 * 2**20
    )(frames)
    to_left = [(i, i - 1) for i in range(1, tiles)]
    to_right = [(i, i + 1) for i in range(tiles - 1)]
    halo_l0 = lax.ppermute(own_l0, "tiles", to_left)
    halo_r0 = lax.ppermute(own_r0, "tiles", to_right)
    halo_l1 = lax.ppermute(own_l1, "tiles", to_left)
    halo_r1 = lax.ppermute(own_r1, "tiles", to_right)

    sums = (2, 4, 3, side, side)
    (before,) = call(start_kernel, [sums], 1, 4, moved_bytes=2**20)(scalars, own_r0, own_r1, right_taper, left_taper)
    (before,) = call(middle_kernel, [sums], 1, 7, flops=2 * 10**9, moved_bytes=8 * 2**20)(
        scalars, own_l0, halo_l0, own_r0, halo_r0, right_taper, left_taper, before
    )
    parted = (2, 2, 3, side, side)
    kept, sent = call(
        last_kernel, [parted, parted], 1, 7, scratch=[pltpu.VMEM(sums, float32)], flops=10**9, moved_bytes=4 * 2**20
    )(scalars, own_l1, halo_l1, own_r1, halo_r1, right_taper, left_taper, before)

    other_core = [(g, g ^ 1) for g in range(4)]
    other_half = [(g, g ^ 2) for g in range(4)]
    got = lax.ppermute(sent, "frames", other_core)
    folded = (2, folded_rows, side)
    here, there = call(fold_kernel, [folded, folded], 1, 3, flops=10**9, moved_bytes=4 * 2**20)(scalars, kept, got, flip)
    here = here + lax.ppermute(there, "tiles", to_left)
    there = lax.ppermute(here, "frames", other_half)

    block = (half, 2 * side)
    upper, lower = call(solve_kernel, [block, block], 2, 9, flops=10**9, moved_bytes=4 * 2**20)(
        scalars,
        factors,
        here,
        there,
        flip,
        right,
        left,
        right_back,
        left_back,
        inverse_eigen_of(shifts),
        window,
    )
    below_other = [(g * tiles + i, (g ^ 1) * tiles + i + 1) for g in range(4) for i in range(tiles - 1)]
    upper_other = lax.ppermute(upper, "frames", other_core)
    lower_own = lax.ppermute(lower, "tiles", to_right)
    lower_other = lax.ppermute(lower, ("frames", "tiles"), below_other)
    (image,) = call(join_kernel, [(half, width)], 1, 4)(scalars, upper, upper_other, lower_own, lower_other)
    return image


def solution(mesh):
    placed = (P("frames", "tiles", None), P("tiles"), P("tiles"), P())
    return jax.shard_map(on_device, mesh=mesh, in_specs=placed, out_specs=P("tiles", None), check_vma=False)
```

```python
import jax
import jax.numpy as jnp
import ml_dtypes
import numpy as np
from jax import lax
from jax.experimental import pallas as pl
from jax.experimental.pallas import tpu as pltpu
from jax.sharding import PartitionSpec as P

ridge_term = 0.1
share_term = 0.0001
tiny_term = 1e-06

side = 128
half = 64
width = 320
quad_width = 4 * width
folded_rows = 200
total_frames = 80
float32 = jnp.float32
bfloat16 = jnp.bfloat16
vmem_limit = 48 * 1024 * 1024


def as_pieces(table):
    upper = table.astype(np.float32).astype(ml_dtypes.bfloat16)
    lower = (table - upper.astype(np.float64)).astype(np.float32).astype(ml_dtypes.bfloat16)
    return upper, lower


def complex_tables():
    index = np.arange(side)
    angle = 2.0 * np.pi * (index[:, None] * index[None, :] % side) / side
    cosine, sine = np.cos(angle), np.sin(angle)
    taper = np.sin(np.pi * (index + 0.5) / side) ** 2
    wc, ws = taper[:, None] * cosine, taper[:, None] * sine
    right_taper = np.block([[wc, -ws], [ws, wc]])
    left_taper = np.block([[wc.T, ws.T], [-ws.T, wc.T]])
    right = np.block([[cosine, -sine], [sine, cosine]])
    left = np.block([[cosine, sine], [-sine, cosine]])
    right_back = np.block([[cosine, sine], [-sine, cosine]])
    left_back = np.block([[cosine, -sine], [sine, cosine]])
    window = (taper[:, None] * taper[None, :] / side**2).astype(np.float32)
    exact = np.stack([right, left, right_back, left_back]).astype(np.float32)
    return [deep(right_taper), wide(left_taper), exact, deep(right_back), wide(left_back), window]


def deep(table):
    upper, lower = as_pieces(table)
    return np.concatenate([upper, upper, lower], axis=0)


def wide(table):
    upper, lower = as_pieces(table)
    return np.concatenate([upper, upper, lower], axis=1)


def pieces(values):
    upper = values.astype(bfloat16)
    lower = (values - upper.astype(float32)).astype(bfloat16)
    return upper, lower


def product(a, b):
    return jnp.dot(a, b, preferred_element_type=float32)


def times_table(values, table):
    upper, lower = pieces(values)
    return product(jnp.concatenate([upper, lower, upper], axis=1), table)


def table_times(table, values):
    upper, lower = pieces(values)
    return product(table, jnp.concatenate([upper, lower, upper], axis=0))


def exactly(a, b):
    return jnp.dot(a, b, precision=lax.Precision.HIGHEST, preferred_element_type=float32)


def upright(g):
    return jnp.concatenate([g[:, :side], g[:, side:]], axis=0)


def moved(values, row_step, col_step):
    return pltpu.roll(pltpu.roll(values, side - col_step, 1), side - row_step, 0)


def moved_back(values, row_step, col_step):
    return pltpu.roll(pltpu.roll(values, col_step, 1), row_step, 0)


def negation(step, twice_axis):
    down = lax.broadcasted_iota(jnp.int32, (side, side), 0)
    across = lax.broadcasted_iota(jnp.int32, (side, side), 1)
    once = jnp.where(((down + across + step) & (side - 1)) == 0, 1.0, 0.0).astype(bfloat16)
    return jnp.concatenate([once, once], axis=twice_axis)


def mirrored(planes, row_step, col_step, rows=side):
    upper, lower = pieces(jnp.concatenate(planes, axis=0))
    tall = product(jnp.concatenate([upper, lower], axis=1), negation(col_step, 0))
    across = jnp.concatenate([tall[i * side : (i + 1) * side] for i in range(len(planes))], axis=1)
    upper, lower = pieces(across)
    across = product(negation(row_step, 1)[:rows], jnp.concatenate([upper, lower], axis=0))
    return [across[:, i * side : (i + 1) * side] for i in range(len(planes))]


def pack_kernel(frames_ref, *out_refs):
    f = 0
    for out_ref in out_refs:
        for quad in range(out_ref.shape[0]):
            for j in range(2):
                one, two = frames_ref[f + j], frames_ref[f + 2 + j]
                base = 2 * width * j
                out_ref[quad, :, base : base + 256] = one[:, :256]
                out_ref[quad, :, base + 256 : base + 512] = two[:, :256]
                out_ref[quad, :, base + 512 : base + 640] = jnp.concatenate([one[:, 256:], two[:, 256:]], axis=1)
            f += 4


def add_quad(upper, lower, row_step, col_step, left, right, spectrum, acc):
    cut = 2 * width
    high, low = pieces(jnp.concatenate([upper[:, :cut], lower[:, :cut], upper[:, cut:], lower[:, cut:]], axis=0))
    g = product(left, jnp.concatenate([high, low, high], axis=0))
    places = []
    for piece in pieces(g):
        column = []
        for p in range(2):
            base = 256 * p
            last = 512 + half * p
            column.append(piece[:, base : base + 128])
            column.append(piece[:, base + half : base + half + 128])
            column.append(piece[:, base + 128 : base + 256])
            column.append(jnp.concatenate([piece[:, base + 192 : base + 256], piece[:, last : last + half]], axis=1))
        places.append(jnp.concatenate([jnp.concatenate([c[:side], c[side:]], axis=1) for c in column], axis=0))
    high, low = places
    z = product(jnp.concatenate([high, low, high], axis=1), right)
    for k in range(8):
        for part in range(2):
            plane = z[k * side : (k + 1) * side, part * side : (part + 1) * side]
            spectrum[k, part, 0:side] = plane
            spectrum[k, part, side : side + half] = plane[:half]
    for c in range(4):
        power, cross_a, cross_b = acc[c, 0], acc[c, 1], acc[c, 2]
        for k in (c, 4 + c):
            zr = z[k * side : (k + 1) * side, :side]
            zi = z[k * side : (k + 1) * side, side:]
            power = power + (zr * zr + zi * zi)
            yr = pltpu.roll(spectrum[k, 0, pl.ds(1, side)], side - col_step, 1)
            yi = pltpu.roll(spectrum[k, 1, pl.ds(1, side)], side - col_step, 1)
            cross_a = cross_a + (zi * yr - zr * yi)
            yr = pltpu.roll(spectrum[k, 0, pl.ds(row_step, side)], side - 1, 1)
            yi = pltpu.roll(spectrum[k, 1, pl.ds(row_step, side)], side - 1, 1)
            cross_b = cross_b + (zi * yr - zr * yi)
        acc[c, 0], acc[c, 1], acc[c, 2] = power, cross_a, cross_b


def number(numbers, i):
    return numbers[i][0, 0]


def fold(acc, row_step, col_step, lower_core, kept, sent):
    lanes = lax.broadcasted_iota(jnp.int32, (half, side), 1)
    top = folded_rows - side
    power = mirrored([acc[c, 0] for c in range(4)], 0, 0, 80)
    cross_a = mirrored([acc[c, 1] for c in range(4)], 1, col_step, half)
    cross_b = mirrored([acc[c, 2] for c in range(4)], row_step, 1)
    planes = []
    for c in range(4):
        total = acc[c, 2] + cross_b[c]
        total = jnp.where(lanes < half, total[:half], pltpu.roll(total[half:], half, 1))
        planes.append((acc[c, 1, :half] + cross_a[c], total, acc[c, 0, :top] + power[c][:top]))
    for j in range(2):
        for one, two, at in zip(planes[j], planes[2 + j], ((0, half), (half, side), (side, folded_rows))):
            kept[j, at[0] : at[1]] = jnp.where(lower_core, one, two)
            sent[j, at[0] : at[1]] = jnp.where(lower_core, two, one)


def start_kernel(numbers, own_r, right_ref, left_ref, out_ref, eigen_ref, spectrum):
    row_step, col_step = number(numbers, 0), number(numbers, 1)
    down = lax.broadcasted_iota(jnp.int32, (side, side), 0)
    across = lax.broadcasted_iota(jnp.int32, (side, side), 1)
    total = jnp.full((side, side), ridge_term, float32)
    for rows, cols in ((1, col_step), (row_step, 1)):
        angle = (down * rows + across * cols) & (side - 1)
        total = total + 2.0 - 2.0 * jnp.cos(angle.astype(float32) * (2.0 * np.pi / side))
    eigen_ref[...] = 1.0 / (total * (side * side))
    out_ref[...] = jnp.zeros_like(out_ref)

    @pl.when(number(numbers, 3) == 1)
    def last_tile():
        blank = jnp.zeros((half, quad_width), float32)

        def body(i, carry):
            add_quad(own_r[i], blank, row_step, col_step, left_ref[...], right_ref[...], spectrum, out_ref)
            return carry

        lax.fori_loop(0, own_r.shape[0], body, 0)


def sum_kernel(numbers, uppers, lowers, right_ref, left_ref, *refs):
    kept, sent, acc, spectrum = refs[-4:]
    row_step, col_step = number(numbers, 0), number(numbers, 1)
    acc[...] = refs[1][...] if len(refs) == 6 else jnp.zeros_like(acc)

    for i in range(uppers.shape[0]):
        add_quad(uppers[i], lowers[i], row_step, col_step, left_ref[...], right_ref[...], spectrum.at[i % 2], acc)
    fold(acc, row_step, col_step, number(numbers, 2) == 0, kept, sent)


def solve_kernel(numbers, here, there, exact, right_back, left_back, inverse_eigen, window, upper_ref, lower_ref):
    row_step, col_step = number(numbers, 0), number(numbers, 1)
    lower_core = number(numbers, 2) == 0
    live_first, live_last = number(numbers, 4), number(numbers, 4) + number(numbers, 5)
    lanes = lax.broadcasted_iota(jnp.int32, (side, side), 1)
    blank = jnp.zeros((half, side), float32)
    powers, crosses_a, crosses_b = [], [], []
    for j in range(2):
        both = here[j] + there[j]
        crowded = both[half:side]
        powers.append(jnp.concatenate([both[side:], blank[: 2 * side - folded_rows]], axis=0))
        crosses_a.append(jnp.concatenate([both[:half], blank], axis=0))
        spread = jnp.concatenate([crowded, pltpu.roll(crowded, half, 1)], axis=0)
        crosses_b.append(jnp.where(lanes < half, spread, 0.0))
    far_powers = mirrored(powers, 0, 0)
    far_a = mirrored(crosses_a, 1, col_step)
    far_b = mirrored(crosses_b, row_step, 1)
    scale = 0.5 / total_frames
    targets, amplitudes = [], []
    for j in range(2):
        power = jnp.concatenate([powers[j][: folded_rows - side], far_powers[j][folded_rows - side :]], axis=0)
        power = power * scale
        cross_a = (crosses_a[j] + far_a[j]) * scale
        cross_b = (crosses_b[j] + far_b[j]) * scale
        level = jnp.sum(jnp.sum(power, axis=0, keepdims=True), axis=1, keepdims=True) * (1.0 / (side * side))
        floor = share_term * level * level
        target = jnp.zeros((side, side), float32)
        for cross, rows, cols in ((cross_a, 1, col_step), (cross_b, row_step, 1)):
            partner = moved(power, rows, cols)
            coherence = cross / (jnp.sqrt(power * partner + floor) + tiny_term)
            target = target + coherence - moved_back(coherence, rows, cols)
        targets.append(target)
        amplitudes.append(jnp.sqrt(power))
    z = exactly(exact[1], upright(exactly(jnp.concatenate(targets, axis=1), exact[0])))
    zr = z[:side] * inverse_eigen[...]
    zi = z[side:] * inverse_eigen[...]
    phase = table_times(left_back[...], upright(times_table(jnp.concatenate([zr, zi], axis=1), right_back[...])))
    cosine, sine = jnp.cos(phase), jnp.sin(phase)
    first, second = amplitudes
    wr = first * cosine[:side] - second * sine[side:]
    wi = first * sine[:side] + second * cosine[side:]
    rebuilt = exactly(exact[3], upright(exactly(jnp.concatenate([wr, wi], axis=1), exact[2])))
    live = []
    for j in range(2):
        c = 2 * number(numbers, 2) + j
        live.append(jnp.where((c >= live_first) & (c < live_last), 1.0, 0.0).astype(float32))
    first = rebuilt[:side] * (window[...] * live[0])
    second = pltpu.roll(rebuilt[side:] * (window[...] * live[1]), half, 1)
    left_part = first + jnp.where(lanes >= half, second, 0.0)
    right_part = jnp.where(lanes < half, second, 0.0)
    for at, part in ((0, left_part), (side, right_part)):
        lower_ref[:, at : at + side] = part[half:]
    place(lower_core, left_part[:half], right_part[:half], upper_ref)


def place(lower_core, left, right, out_ref):
    out_ref[:, 0:128] = jnp.where(lower_core, left, 0.0)
    out_ref[:, 128:256] = jnp.where(lower_core, right, left)
    out_ref[:, 256:320] = jnp.where(lower_core, 0.0, right)[:, :half]


def receive_kernel(numbers, upper, lower, out_ref):
    place(number(numbers, 2) == 0, lower[:, :side], lower[:, side:], out_ref)
    out_ref[...] += upper[...]


vmem = pl.BlockSpec(memory_space=pltpu.VMEM)


def shape_of(dims, dtype=float32):
    return jax.ShapeDtypeStruct(dims, dtype)


def call(kernel, shapes, array_count, scratch=(), flops=0, moved_bytes=0):
    return pl.pallas_call(
        kernel,
        out_shape=shapes,
        in_specs=[vmem] * array_count,
        out_specs=[vmem] * len(shapes),
        scratch_shapes=list(scratch),
        compiler_params=pltpu.CompilerParams(vmem_limit_bytes=vmem_limit),
        cost_estimate=pl.CostEstimate(flops=flops, bytes_accessed=moved_bytes, transcendentals=0),
    )


def on_device(frames, live_first, live_count, shifts):
    tiles = lax.axis_size("tiles")
    tile = lax.axis_index("tiles")
    core = lax.axis_index("frames") % 2
    right_taper, left_taper, exact, right_back, left_back, window = [jnp.asarray(t) for t in complex_tables()]
    numbers = jnp.stack([shifts[1, 0], shifts[0, 1], core, tile == tiles - 1, live_first[0], live_count[0]])
    numbers = jnp.broadcast_to(numbers.astype(jnp.int32)[:, None, None], (6, 8, side))

    to_left = [(i, i - 1) for i in range(1, tiles)]
    to_right = [(i, i + 1) for i in range(tiles - 1)]
    other_core = [(g, g ^ 1) for g in range(4)]
    other_half = [(g, g ^ 2) for g in range(4)]
    count_r = 8
    count_l = frames.shape[0] - count_r
    packed = [shape_of((n // 4, half, quad_width)) for n in (count_l, count_r)]
    own_l, own_r = call(pack_kernel, packed, 1)(frames)
    halo_l = lax.ppermute(own_l, "tiles", to_left)
    halo_r = lax.ppermute(own_r, "tiles", to_right)

    sums, folded = (4, 3, side, side), shape_of((2, folded_rows, side))
    spectrum = pltpu.VMEM((8, 2, side + half, side), float32)
    scratch = [pltpu.VMEM(sums, float32), pltpu.VMEM((2, 8, 2, side + half, side), float32)]
    before, inverse_eigen = call(start_kernel, [shape_of(sums), shape_of((side, side))], 4, [spectrum], 16 * 10**9)(
        numbers, own_r, right_taper, left_taper
    )
    kept, sent = call(sum_kernel, [folded, folded], 6, scratch)(
        numbers, halo_r, own_r, right_taper, left_taper, inverse_eigen
    )
    away = kept + lax.ppermute(sent, "frames", other_core)
    back = lax.ppermute(away, "tiles", to_left)
    kept, sent = call(sum_kernel, [folded, folded], 7, scratch)(
        numbers, own_l, halo_l, right_taper, left_taper, away, before
    )
    here = kept + back + lax.ppermute(sent, "frames", other_core)
    there = lax.ppermute(here, "frames", other_half)

    block = shape_of((half, width))
    upper, lower = call(solve_kernel, [block, shape_of((half, 2 * side))], 8)(
        numbers, here, there, exact, right_back, left_back, inverse_eigen, window
    )
    lower = lax.ppermute(lower, "tiles", to_right)
    (own,) = call(receive_kernel, [block], 3)(numbers, upper, lower)
    return own + lax.ppermute(own, "frames", other_core)


def solution(mesh):
    placed = (P("frames", "tiles", None), P("tiles"), P("tiles"), P())
    return jax.shard_map(on_device, mesh=mesh, in_specs=placed, out_specs=P("tiles", None), check_vma=False)
```

```python
import jax
import jax.numpy as jnp
import ml_dtypes
import numpy as np
from jax import lax
from jax.experimental import pallas as pl
from jax.experimental.pallas import tpu as pltpu
from jax.sharding import PartitionSpec as P

ridge_term = 0.1
share_term = 0.0001
tiny_term = 1e-06

side = 128
half = 64
width = 320
quad_width = 4 * width
folded_rows = 200
total_frames = 80
float32 = jnp.float32
bfloat16 = jnp.bfloat16
vmem_limit = 48 * 1024 * 1024


def as_pieces(table):
    upper = table.astype(np.float32).astype(ml_dtypes.bfloat16)
    lower = (table - upper.astype(np.float64)).astype(np.float32).astype(ml_dtypes.bfloat16)
    return upper, lower


def complex_tables():
    index = np.arange(side)
    angle = 2.0 * np.pi * (index[:, None] * index[None, :] % side) / side
    cosine, sine = np.cos(angle), np.sin(angle)
    taper = np.sin(np.pi * (index + 0.5) / side) ** 2
    wc, ws = taper[:, None] * cosine, taper[:, None] * sine
    right_taper = np.block([[wc, -ws], [ws, wc]])
    left_taper = np.block([[wc.T, ws.T], [-ws.T, wc.T]])
    right = np.block([[cosine, -sine], [sine, cosine]])
    left = np.block([[cosine, sine], [-sine, cosine]])
    right_back = np.block([[cosine, sine], [-sine, cosine]])
    left_back = np.block([[cosine, -sine], [sine, cosine]])
    window = (taper[:, None] * taper[None, :] / side**2).astype(np.float32)
    exact = np.stack([right, left, right_back, left_back]).astype(np.float32)
    rows = np.concatenate([index[:half], side + index[:half]])
    tapers = [deep(right_taper), wide(left_taper[:, rows]), wide(left_taper[:, rows + half])]
    return [*tapers, exact, deep(right_back), wide(left_back), window]


def deep(table):
    upper, lower = as_pieces(table)
    return np.concatenate([upper, upper, lower], axis=0)


def wide(table):
    upper, lower = as_pieces(table)
    return np.concatenate([upper, upper, lower], axis=1)


def pieces(values):
    upper = values.astype(bfloat16)
    lower = (values - upper.astype(float32)).astype(bfloat16)
    return upper, lower


def product(a, b):
    return jnp.dot(a, b, preferred_element_type=float32)


def times_table(values, table):
    upper, lower = pieces(values)
    return product(jnp.concatenate([upper, lower, upper], axis=1), table)


def table_times(table, values):
    upper, lower = pieces(values)
    return product(table, jnp.concatenate([upper, lower, upper], axis=0))


def exactly(a, b):
    return jnp.dot(a, b, precision=lax.Precision.HIGHEST, preferred_element_type=float32)


def upright(g):
    return jnp.concatenate([g[:, :side], g[:, side:]], axis=0)


def moved(values, row_step, col_step):
    return pltpu.roll(pltpu.roll(values, side - col_step, 1), side - row_step, 0)


def moved_back(values, row_step, col_step):
    return pltpu.roll(pltpu.roll(values, col_step, 1), row_step, 0)


def negation(step, twice_axis):
    down = lax.broadcasted_iota(jnp.int32, (side, side), 0)
    across = lax.broadcasted_iota(jnp.int32, (side, side), 1)
    once = jnp.where(((down + across + step) & (side - 1)) == 0, 1.0, 0.0).astype(bfloat16)
    return jnp.concatenate([once, once], axis=twice_axis)


def mirrored(planes, row_step, col_step, rows=side):
    upper, lower = pieces(jnp.concatenate(planes, axis=0))
    tall = product(jnp.concatenate([upper, lower], axis=1), negation(col_step, 0))
    across = jnp.concatenate([tall[i * side : (i + 1) * side] for i in range(len(planes))], axis=1)
    upper, lower = pieces(across)
    across = product(negation(row_step, 1)[:rows], jnp.concatenate([upper, lower], axis=0))
    return [across[:, i * side : (i + 1) * side] for i in range(len(planes))]


def pack_kernel(frames_ref, *out_refs):
    f = 0
    for out_ref in out_refs:
        for quad in range(out_ref.shape[0]):
            for j in range(2):
                one, two = frames_ref[f + j], frames_ref[f + 2 + j]
                base = 2 * width * j
                out_ref[quad, :, base : base + 256] = one[:, :256]
                out_ref[quad, :, base + 256 : base + 512] = two[:, :256]
                out_ref[quad, :, base + 512 : base + 640] = jnp.concatenate([one[:, 256:], two[:, 256:]], axis=1)
            f += 4


def rows_of(block, table):
    high, low = pieces(jnp.concatenate([block[:, : 2 * width], block[:, 2 * width :]], axis=0))
    return product(table, jnp.concatenate([high, low, high], axis=0))


def add_quad(g, row_step, col_step, right, spectrum, acc):
    places = []
    for piece in pieces(g):
        column = []
        for p in range(2):
            base = 256 * p
            last = 512 + half * p
            column.append(piece[:, base : base + 128])
            column.append(piece[:, base + half : base + half + 128])
            column.append(piece[:, base + 128 : base + 256])
            column.append(jnp.concatenate([piece[:, base + 192 : base + 256], piece[:, last : last + half]], axis=1))
        places.append(jnp.concatenate([jnp.concatenate([c[:side], c[side:]], axis=1) for c in column], axis=0))
    high, low = places
    z = product(jnp.concatenate([high, low, high], axis=1), right)
    for k in range(8):
        for part in range(2):
            plane = z[k * side : (k + 1) * side, part * side : (part + 1) * side]
            spectrum[k, part, 0:side] = plane
            spectrum[k, part, side : side + half] = plane[:half]
    for c in range(4):
        power, cross_a, cross_b = acc[c, 0], acc[c, 1], acc[c, 2]
        for k in (c, 4 + c):
            zr = z[k * side : (k + 1) * side, :side]
            zi = z[k * side : (k + 1) * side, side:]
            power = power + (zr * zr + zi * zi)
            yr = pltpu.roll(spectrum[k, 0, pl.ds(1, side)], side - col_step, 1)
            yi = pltpu.roll(spectrum[k, 1, pl.ds(1, side)], side - col_step, 1)
            cross_a = cross_a + (zi * yr - zr * yi)
            yr = pltpu.roll(spectrum[k, 0, pl.ds(row_step, side)], side - 1, 1)
            yi = pltpu.roll(spectrum[k, 1, pl.ds(row_step, side)], side - 1, 1)
            cross_b = cross_b + (zi * yr - zr * yi)
        acc[c, 0], acc[c, 1], acc[c, 2] = power, cross_a, cross_b


def number(numbers, i):
    return numbers[i][0, 0]


def fold(acc, row_step, col_step, lower_core, kept, sent):
    lanes = lax.broadcasted_iota(jnp.int32, (half, side), 1)
    top = folded_rows - side
    power = mirrored([acc[c, 0] for c in range(4)], 0, 0, 80)
    cross_a = mirrored([acc[c, 1] for c in range(4)], 1, col_step, half)
    cross_b = mirrored([acc[c, 2] for c in range(4)], row_step, 1)
    planes = []
    for c in range(4):
        total = acc[c, 2] + cross_b[c]
        total = jnp.where(lanes < half, total[:half], pltpu.roll(total[half:], half, 1))
        planes.append((acc[c, 1, :half] + cross_a[c], total, acc[c, 0, :top] + power[c][:top]))
    for j in range(2):
        for one, two, at in zip(planes[j], planes[2 + j], ((0, half), (half, side), (side, folded_rows))):
            kept[j, at[0] : at[1]] = jnp.where(lower_core, one, two)
            sent[j, at[0] : at[1]] = jnp.where(lower_core, two, one)


def start_kernel(
    numbers, own_l, own_r, right_ref, upper_ref, lower_ref, out_ref, eigen_ref, rows_l_ref, rows_r_ref, spectrum
):
    row_step, col_step = number(numbers, 0), number(numbers, 1)
    down = lax.broadcasted_iota(jnp.int32, (side, side), 0)
    across = lax.broadcasted_iota(jnp.int32, (side, side), 1)
    total = jnp.full((side, side), ridge_term, float32)
    for rows, cols in ((1, col_step), (row_step, 1)):
        angle = (down * rows + across * cols) & (side - 1)
        total = total + 2.0 - 2.0 * jnp.cos(angle.astype(float32) * (2.0 * np.pi / side))
    eigen_ref[...] = 1.0 / (total * (side * side))
    out_ref[...] = jnp.zeros_like(out_ref)
    for i in range(own_l.shape[0]):
        rows_l_ref[i] = rows_of(own_l[i], upper_ref[...])
    for i in range(own_r.shape[0]):
        rows_r_ref[i] = rows_of(own_r[i], lower_ref[...])

    @pl.when(number(numbers, 3) == 1)
    def last_tile():
        def body(i, carry):
            add_quad(rows_of(own_r[i], upper_ref[...]), row_step, col_step, right_ref[...], spectrum, out_ref)
            return carry

        lax.fori_loop(0, own_r.shape[0], body, 0)


def sum_kernel(numbers, own, halo, right_ref, left_ref, *refs):
    kept, sent, acc, spectrum = refs[-4:]
    row_step, col_step = number(numbers, 0), number(numbers, 1)
    acc[...] = refs[1][...] if len(refs) == 6 else jnp.zeros_like(acc)
    for i in range(halo.shape[0]):
        g = own[i] + rows_of(halo[i], left_ref[...])
        add_quad(g, row_step, col_step, right_ref[...], spectrum.at[i % 2], acc)
    fold(acc, row_step, col_step, number(numbers, 2) == 0, kept, sent)


def wave(angle):
    turns = jnp.floor(angle * (2.0 / np.pi) + 0.5)
    rest = angle - turns * np.float32(1.5703125)
    rest = rest - turns * np.float32(4.837512969970703125e-4)
    rest = rest - turns * np.float32(7.549789948768648e-8)
    square = rest * rest
    sine = rest + rest * square * (-1.6666654611e-1 + square * (8.3321608736e-3 - square * 1.9515295891e-4))
    cosine = 1.0 - 0.5 * square + square * square * (4.166664568298827e-2 + square * (-1.388731625493765e-3 + square * 2.443315711809948e-5))
    quarter = turns.astype(jnp.int32)
    odd = (quarter & 1) == 1
    first = jnp.where(odd, sine, cosine)
    second = jnp.where(odd, cosine, sine)
    first = jnp.where(((quarter + 1) & 2) == 2, -first, first)
    second = jnp.where((quarter & 2) == 2, -second, second)
    return first, second


def solve_kernel(numbers, here, there, exact, right_back, left_back, inverse_eigen, window, upper_ref, lower_ref):
    row_step, col_step = number(numbers, 0), number(numbers, 1)
    lower_core = number(numbers, 2) == 0
    live_first, live_last = number(numbers, 4), number(numbers, 4) + number(numbers, 5)
    lanes = lax.broadcasted_iota(jnp.int32, (side, side), 1)
    blank = jnp.zeros((half, side), float32)
    powers, crosses_a, crosses_b = [], [], []
    for j in range(2):
        both = here[j] + there[j]
        crowded = both[half:side]
        powers.append(jnp.concatenate([both[side:], blank[: 2 * side - folded_rows]], axis=0))
        crosses_a.append(jnp.concatenate([both[:half], blank], axis=0))
        spread = jnp.concatenate([crowded, pltpu.roll(crowded, half, 1)], axis=0)
        crosses_b.append(jnp.where(lanes < half, spread, 0.0))
    far_powers = mirrored(powers, 0, 0)
    far_a = mirrored(crosses_a, 1, col_step)
    far_b = mirrored(crosses_b, row_step, 1)
    scale = 0.5 / total_frames
    targets, amplitudes = [], []
    for j in range(2):
        power = jnp.concatenate([powers[j][: folded_rows - side], far_powers[j][folded_rows - side :]], axis=0)
        power = power * scale
        cross_a = (crosses_a[j] + far_a[j]) * scale
        cross_b = (crosses_b[j] + far_b[j]) * scale
        level = jnp.sum(jnp.sum(power, axis=0, keepdims=True), axis=1, keepdims=True) * (1.0 / (side * side))
        floor = share_term * level * level
        target = jnp.zeros((side, side), float32)
        for cross, rows, cols in ((cross_a, 1, col_step), (cross_b, row_step, 1)):
            partner = moved(power, rows, cols)
            coherence = cross / (jnp.sqrt(power * partner + floor) + tiny_term)
            target = target + coherence - moved_back(coherence, rows, cols)
        targets.append(target)
        amplitudes.append(jnp.sqrt(power))
    z = exactly(exact[1], upright(exactly(jnp.concatenate(targets, axis=1), exact[0])))
    zr = z[:side] * inverse_eigen[...]
    zi = z[side:] * inverse_eigen[...]
    phase = table_times(left_back[...], upright(times_table(jnp.concatenate([zr, zi], axis=1), right_back[...])))
    cosine, sine = wave(phase)
    first, second = amplitudes
    wr = first * cosine[:side] - second * sine[side:]
    wi = first * sine[:side] + second * cosine[side:]
    rebuilt = exactly(exact[3], upright(exactly(jnp.concatenate([wr, wi], axis=1), exact[2])))
    live = []
    for j in range(2):
        c = 2 * number(numbers, 2) + j
        live.append(jnp.where((c >= live_first) & (c < live_last), 1.0, 0.0).astype(float32))
    first = rebuilt[:side] * (window[...] * live[0])
    second = pltpu.roll(rebuilt[side:] * (window[...] * live[1]), half, 1)
    left_part = first + jnp.where(lanes >= half, second, 0.0)
    right_part = jnp.where(lanes < half, second, 0.0)
    for at, part in ((0, left_part), (side, right_part)):
        lower_ref[:, at : at + side] = part[half:]
    place(lower_core, left_part[:half], right_part[:half], upper_ref)


def place(lower_core, left, right, out_ref):
    out_ref[:, 0:128] = jnp.where(lower_core, left, 0.0)
    out_ref[:, 128:256] = jnp.where(lower_core, right, left)
    out_ref[:, 256:320] = jnp.where(lower_core, 0.0, right)[:, :half]


def receive_kernel(numbers, upper, lower, out_ref):
    place(number(numbers, 2) == 0, lower[:, :side], lower[:, side:], out_ref)
    out_ref[...] += upper[...]


vmem = pl.BlockSpec(memory_space=pltpu.VMEM)


def shape_of(dims, dtype=float32):
    return jax.ShapeDtypeStruct(dims, dtype)


def call(kernel, shapes, array_count, scratch=(), flops=0, moved_bytes=0):
    return pl.pallas_call(
        kernel,
        out_shape=shapes,
        in_specs=[vmem] * array_count,
        out_specs=[vmem] * len(shapes),
        scratch_shapes=list(scratch),
        compiler_params=pltpu.CompilerParams(vmem_limit_bytes=vmem_limit),
        cost_estimate=pl.CostEstimate(flops=flops, bytes_accessed=moved_bytes, transcendentals=0),
    )


def on_device(frames, live_first, live_count, shifts):
    tiles = lax.axis_size("tiles")
    tile = lax.axis_index("tiles")
    core = lax.axis_index("frames") % 2
    right_taper, upper_taper, lower_taper, exact, right_back, left_back, window = [jnp.asarray(t) for t in complex_tables()]
    numbers = jnp.stack([shifts[1, 0], shifts[0, 1], core, tile == tiles - 1, live_first[0], live_count[0]])
    numbers = jnp.broadcast_to(numbers.astype(jnp.int32)[:, None, None], (6, 8, side))

    to_left = [(i, i - 1) for i in range(1, tiles)]
    to_right = [(i, i + 1) for i in range(tiles - 1)]
    other_core = [(g, g ^ 1) for g in range(4)]
    other_half = [(g, g ^ 2) for g in range(4)]
    count_r = 8
    count_l = frames.shape[0] - count_r
    packed = [shape_of((n // 4, half, quad_width)) for n in (count_l, count_r)]
    own_l, own_r = call(pack_kernel, packed, 1)(frames)
    halo_l = lax.ppermute(own_l, "tiles", to_left)
    halo_r = lax.ppermute(own_r, "tiles", to_right)

    sums, folded = (4, 3, side, side), shape_of((2, folded_rows, side))
    spectrum = pltpu.VMEM((8, 2, side + half, side), float32)
    scratch = [pltpu.VMEM(sums, float32), pltpu.VMEM((2, 8, 2, side + half, side), float32)]
    tables = [shape_of(sums), shape_of((side, side))]
    tables += [shape_of((n // 4, 2 * side, 2 * width)) for n in (count_l, count_r)]
    before, inverse_eigen, rows_l, rows_r = call(start_kernel, tables, 6, [spectrum], 16 * 10**9)(
        numbers, own_l, own_r, right_taper, upper_taper, lower_taper
    )
    kept, sent = call(sum_kernel, [folded, folded], 6, scratch)(
        numbers, rows_r, halo_r, right_taper, upper_taper, inverse_eigen
    )
    away = kept + lax.ppermute(sent, "frames", other_core)
    back = lax.ppermute(away, "tiles", to_left)
    kept, sent = call(sum_kernel, [folded, folded], 7, scratch)(
        numbers, rows_l, halo_l, right_taper, lower_taper, away, before
    )
    here = kept + back + lax.ppermute(sent, "frames", other_core)
    there = lax.ppermute(here, "frames", other_half)

    block = shape_of((half, width))
    upper, lower = call(solve_kernel, [block, shape_of((half, 2 * side))], 8)(
        numbers, here, there, exact, right_back, left_back, inverse_eigen, window
    )
    lower = lax.ppermute(lower, "tiles", to_right)
    (own,) = call(receive_kernel, [block], 3)(numbers, upper, lower)
    return own + lax.ppermute(own, "frames", other_core)


def solution(mesh):
    placed = (P("frames", "tiles", None), P("tiles"), P("tiles"), P())
    return jax.shard_map(on_device, mesh=mesh, in_specs=placed, out_specs=P("tiles", None), check_vma=False)
```

```python
import jax
import jax.numpy as jnp
import ml_dtypes
import numpy as np
from jax import lax
from jax.experimental import pallas as pl
from jax.experimental.pallas import tpu as pltpu
from jax.sharding import PartitionSpec as P

ridge_term = 0.1
share_term = 0.0001
tiny_term = 1e-06

side = 128
half = 64
width = 320
quad_width = 4 * width
folded_rows = 200
total_frames = 80
float32 = jnp.float32
bfloat16 = jnp.bfloat16
vmem_limit = 24 * 1024 * 1024


def as_pieces(table):
    upper = table.astype(np.float32).astype(ml_dtypes.bfloat16)
    lower = (table - upper.astype(np.float64)).astype(np.float32).astype(ml_dtypes.bfloat16)
    return upper, lower


def complex_tables():
    index = np.arange(side)
    angle = 2.0 * np.pi * (index[:, None] * index[None, :] % side) / side
    cosine, sine = np.cos(angle), np.sin(angle)
    taper = np.sin(np.pi * (index + 0.5) / side) ** 2
    wc, ws = taper[:, None] * cosine, taper[:, None] * sine
    right_taper = np.block([[wc, -ws], [ws, wc]])
    left_taper = np.block([[wc.T, ws.T], [-ws.T, wc.T]])
    right = np.block([[cosine, -sine], [sine, cosine]])
    left = np.block([[cosine, sine], [-sine, cosine]])
    right_back = np.block([[cosine, sine], [-sine, cosine]])
    left_back = np.block([[cosine, -sine], [sine, cosine]])
    window = (taper[:, None] * taper[None, :] / side**2).astype(np.float32)
    exact = np.stack([right, left, right_back, left_back]).astype(np.float32)
    rows = np.concatenate([index[:half], side + index[:half]])
    tapers = [deep(right_taper), wide(left_taper[:, rows]), wide(left_taper[:, rows + half])]
    return [*tapers, exact, deep(right_back), wide(left_back), window]


def deep(table):
    upper, lower = as_pieces(table)
    return np.concatenate([upper, upper, lower], axis=0)


def wide(table):
    upper, lower = as_pieces(table)
    return np.concatenate([upper, upper, lower], axis=1)


def pieces(values):
    upper = values.astype(bfloat16)
    lower = (values - upper.astype(float32)).astype(bfloat16)
    return upper, lower


def product(a, b):
    return jnp.dot(a, b, preferred_element_type=float32)


def times_table(values, table):
    upper, lower = pieces(values)
    return product(jnp.concatenate([upper, lower, upper], axis=1), table)


def table_times(table, values):
    upper, lower = pieces(values)
    return product(table, jnp.concatenate([upper, lower, upper], axis=0))


def exactly(a, b):
    return jnp.dot(a, b, precision=lax.Precision.HIGHEST, preferred_element_type=float32)


def upright(g):
    return jnp.concatenate([g[:, :side], g[:, side:]], axis=0)


def moved(values, row_step, col_step):
    return pltpu.roll(pltpu.roll(values, side - col_step, 1), side - row_step, 0)


def moved_back(values, row_step, col_step):
    return pltpu.roll(pltpu.roll(values, col_step, 1), row_step, 0)


def negation(step, twice_axis):
    down = lax.broadcasted_iota(jnp.int32, (side, side), 0)
    across = lax.broadcasted_iota(jnp.int32, (side, side), 1)
    once = jnp.where(((down + across + step) & (side - 1)) == 0, 1.0, 0.0).astype(bfloat16)
    return jnp.concatenate([once, once], axis=twice_axis)


def mirrored(planes, row_step, col_step, rows=side):
    upper, lower = pieces(jnp.concatenate(planes, axis=0))
    tall = product(jnp.concatenate([upper, lower], axis=1), negation(col_step, 0))
    across = jnp.concatenate([tall[i * side : (i + 1) * side] for i in range(len(planes))], axis=1)
    upper, lower = pieces(across)
    across = product(negation(row_step, 1)[:rows], jnp.concatenate([upper, lower], axis=0))
    return [across[:, i * side : (i + 1) * side] for i in range(len(planes))]


def pack_kernel(frames_ref, *out_refs):
    f = 0
    for out_ref in out_refs:
        for quad in range(out_ref.shape[0]):
            for j in range(2):
                one, two = frames_ref[f + j], frames_ref[f + 2 + j]
                base = 2 * width * j
                out_ref[quad, :, base : base + 256] = one[:, :256]
                out_ref[quad, :, base + 256 : base + 512] = two[:, :256]
                out_ref[quad, :, base + 512 : base + 640] = jnp.concatenate([one[:, 256:], two[:, 256:]], axis=1)
            f += 4


def rows_of(block, table):
    high, low = pieces(jnp.concatenate([block[:, : 2 * width], block[:, 2 * width :]], axis=0))
    return product(table, jnp.concatenate([high, low, high], axis=0))


def add_quad(g, row_step, col_step, right, spectrum, acc):
    places = []
    for piece in pieces(g):
        column = []
        for p in range(2):
            base = 256 * p
            last = 512 + half * p
            column.append(piece[:, base : base + 128])
            column.append(piece[:, base + half : base + half + 128])
            column.append(piece[:, base + 128 : base + 256])
            column.append(jnp.concatenate([piece[:, base + 192 : base + 256], piece[:, last : last + half]], axis=1))
        places.append(jnp.concatenate([jnp.concatenate([c[:side], c[side:]], axis=1) for c in column], axis=0))
    high, low = places
    z = product(jnp.concatenate([high, low, high], axis=1), right)
    for k in range(8):
        for part in range(2):
            plane = z[k * side : (k + 1) * side, part * side : (part + 1) * side]
            spectrum[k, part, 0:side] = plane
            spectrum[k, part, side : side + half] = plane[:half]
    for c in range(4):
        power, cross_a, cross_b = acc[c, 0], acc[c, 1], acc[c, 2]
        for k in (c, 4 + c):
            zr = z[k * side : (k + 1) * side, :side]
            zi = z[k * side : (k + 1) * side, side:]
            power = power + (zr * zr + zi * zi)
            yr = pltpu.roll(spectrum[k, 0, pl.ds(1, side)], side - col_step, 1)
            yi = pltpu.roll(spectrum[k, 1, pl.ds(1, side)], side - col_step, 1)
            cross_a = cross_a + (zi * yr - zr * yi)
            yr = pltpu.roll(spectrum[k, 0, pl.ds(row_step, side)], side - 1, 1)
            yi = pltpu.roll(spectrum[k, 1, pl.ds(row_step, side)], side - 1, 1)
            cross_b = cross_b + (zi * yr - zr * yi)
        acc[c, 0], acc[c, 1], acc[c, 2] = power, cross_a, cross_b


def number(numbers, i):
    return numbers[i][0, 0]


def fold(acc, row_step, col_step, lower_core, kept, sent):
    lanes = lax.broadcasted_iota(jnp.int32, (half, side), 1)
    top = folded_rows - side
    power = mirrored([acc[c, 0] for c in range(4)], 0, 0, 80)
    cross_a = mirrored([acc[c, 1] for c in range(4)], 1, col_step, half)
    cross_b = mirrored([acc[c, 2] for c in range(4)], row_step, 1)
    planes = []
    for c in range(4):
        total = acc[c, 2] + cross_b[c]
        total = jnp.where(lanes < half, total[:half], pltpu.roll(total[half:], half, 1))
        planes.append((acc[c, 1, :half] + cross_a[c], total, acc[c, 0, :top] + power[c][:top]))
    for j in range(2):
        for one, two, at in zip(planes[j], planes[2 + j], ((0, half), (half, side), (side, folded_rows))):
            kept[j, at[0] : at[1]] = jnp.where(lower_core, one, two)
            sent[j, at[0] : at[1]] = jnp.where(lower_core, two, one)


def start_kernel(
    numbers, own_l, own_r, right_ref, upper_ref, lower_ref, out_ref, eigen_ref, rows_l_ref, rows_r_ref, spectrum
):
    row_step, col_step = number(numbers, 0), number(numbers, 1)
    down = lax.broadcasted_iota(jnp.int32, (side, side), 0)
    across = lax.broadcasted_iota(jnp.int32, (side, side), 1)
    total = jnp.full((side, side), ridge_term, float32)
    for rows, cols in ((1, col_step), (row_step, 1)):
        angle = (down * rows + across * cols) & (side - 1)
        total = total + 2.0 - 2.0 * jnp.cos(angle.astype(float32) * (2.0 * np.pi / side))
    eigen_ref[...] = 1.0 / (total * (side * side))
    out_ref[...] = jnp.zeros_like(out_ref)
    for i in range(own_l.shape[0]):
        rows_l_ref[i] = rows_of(own_l[i], upper_ref[...])
    for i in range(own_r.shape[0]):
        rows_r_ref[i] = rows_of(own_r[i], lower_ref[...])

    @pl.when(number(numbers, 3) == 1)
    def last_tile():
        def body(i, carry):
            add_quad(rows_of(own_r[i], upper_ref[...]), row_step, col_step, right_ref[...], spectrum, out_ref)
            return carry

        lax.fori_loop(0, own_r.shape[0], body, 0)


def sum_kernel(numbers, own, halo, right_ref, left_ref, *refs):
    kept, sent, acc, spectrum = refs[-4:]
    row_step, col_step = number(numbers, 0), number(numbers, 1)
    acc[...] = refs[1][...] if len(refs) == 6 else jnp.zeros_like(acc)
    for i in range(halo.shape[0]):
        g = own[i] + rows_of(halo[i], left_ref[...])
        add_quad(g, row_step, col_step, right_ref[...], spectrum.at[i % 2], acc)
    fold(acc, row_step, col_step, number(numbers, 2) == 0, kept, sent)


def wave(angle):
    turns = jnp.floor(angle * (2.0 / np.pi) + 0.5)
    rest = angle - turns * np.float32(1.5703125)
    rest = rest - turns * np.float32(4.837512969970703125e-4)
    rest = rest - turns * np.float32(7.549789948768648e-8)
    square = rest * rest
    sine = rest + rest * square * (-1.6666654611e-1 + square * (8.3321608736e-3 - square * 1.9515295891e-4))
    cosine = 1.0 - 0.5 * square + square * square * (4.166664568298827e-2 + square * (-1.388731625493765e-3 + square * 2.443315711809948e-5))
    quarter = turns.astype(jnp.int32)
    odd = (quarter & 1) == 1
    first = jnp.where(odd, sine, cosine)
    second = jnp.where(odd, cosine, sine)
    first = jnp.where(((quarter + 1) & 2) == 2, -first, first)
    second = jnp.where((quarter & 2) == 2, -second, second)
    return first, second


def total_kernel(numbers, both, *refs):
    total = jnp.where(number(numbers, 2) == 0, both[1], both[0])
    for ref in refs[:-1]:
        total = total + ref[...]
    refs[-1][...] = total


def solve_kernel(numbers, halves, exact, right_back, left_back, inverse_eigen, window, upper_ref, lower_ref):
    row_step, col_step = number(numbers, 0), number(numbers, 1)
    lower_core = number(numbers, 2) == 0
    live_first, live_last = number(numbers, 4), number(numbers, 4) + number(numbers, 5)
    lanes = lax.broadcasted_iota(jnp.int32, (side, side), 1)
    blank = jnp.zeros((half, side), float32)
    powers, crosses_a, crosses_b = [], [], []
    for j in range(2):
        both = halves[0, j] + halves[1, j]
        crowded = both[half:side]
        powers.append(jnp.concatenate([both[side:], blank[: 2 * side - folded_rows]], axis=0))
        crosses_a.append(jnp.concatenate([both[:half], blank], axis=0))
        spread = jnp.concatenate([crowded, pltpu.roll(crowded, half, 1)], axis=0)
        crosses_b.append(jnp.where(lanes < half, spread, 0.0))
    far_powers = mirrored(powers, 0, 0)
    far_a = mirrored(crosses_a, 1, col_step)
    far_b = mirrored(crosses_b, row_step, 1)
    scale = 0.5 / total_frames
    targets, amplitudes = [], []
    for j in range(2):
        power = jnp.concatenate([powers[j][: folded_rows - side], far_powers[j][folded_rows - side :]], axis=0)
        power = power * scale
        cross_a = (crosses_a[j] + far_a[j]) * scale
        cross_b = (crosses_b[j] + far_b[j]) * scale
        level = jnp.sum(jnp.sum(power, axis=0, keepdims=True), axis=1, keepdims=True) * (1.0 / (side * side))
        floor = share_term * level * level
        target = jnp.zeros((side, side), float32)
        for cross, rows, cols in ((cross_a, 1, col_step), (cross_b, row_step, 1)):
            partner = moved(power, rows, cols)
            coherence = cross / (jnp.sqrt(power * partner + floor) + tiny_term)
            target = target + coherence - moved_back(coherence, rows, cols)
        targets.append(target)
        amplitudes.append(jnp.sqrt(power))
    z = exactly(exact[1], upright(exactly(jnp.concatenate(targets, axis=1), exact[0])))
    zr = z[:side] * inverse_eigen[...]
    zi = z[side:] * inverse_eigen[...]
    phase = table_times(left_back[...], upright(times_table(jnp.concatenate([zr, zi], axis=1), right_back[...])))
    cosine, sine = wave(phase)
    first, second = amplitudes
    wr = first * cosine[:side] - second * sine[side:]
    wi = first * sine[:side] + second * cosine[side:]
    rebuilt = exactly(exact[3], upright(exactly(jnp.concatenate([wr, wi], axis=1), exact[2])))
    live = []
    for j in range(2):
        c = 2 * number(numbers, 2) + j
        live.append(jnp.where((c >= live_first) & (c < live_last), 1.0, 0.0).astype(float32))
    first = rebuilt[:side] * (window[...] * live[0])
    second = pltpu.roll(rebuilt[side:] * (window[...] * live[1]), half, 1)
    left_part = first + jnp.where(lanes >= half, second, 0.0)
    right_part = jnp.where(lanes < half, second, 0.0)
    for at, part in ((0, left_part), (side, right_part)):
        lower_ref[:, at : at + side] = part[half:]
    place(lower_core, left_part[:half], right_part[:half], upper_ref)


def place(lower_core, left, right, out_ref):
    out_ref[:, 0:128] = jnp.where(lower_core, left, 0.0)
    out_ref[:, 128:256] = jnp.where(lower_core, right, left)
    out_ref[:, 256:320] = jnp.where(lower_core, 0.0, right)[:, :half]


def receive_kernel(numbers, upper, lower, out_ref):
    place(number(numbers, 2) == 0, lower[:, :side], lower[:, side:], out_ref)
    out_ref[...] += upper[...]


vmem = pl.BlockSpec(memory_space=pltpu.VMEM)


def shape_of(dims, dtype=float32):
    return jax.ShapeDtypeStruct(dims, dtype)


def call(kernel, shapes, array_count, scratch=(), flops=0, moved_bytes=0):
    return pl.pallas_call(
        kernel,
        out_shape=shapes,
        in_specs=[vmem] * array_count,
        out_specs=[vmem] * len(shapes),
        scratch_shapes=list(scratch),
        compiler_params=pltpu.CompilerParams(vmem_limit_bytes=vmem_limit),
        cost_estimate=pl.CostEstimate(flops=flops, bytes_accessed=moved_bytes, transcendentals=0),
    )


def on_device(frames, live_first, live_count, shifts):
    tiles = lax.axis_size("tiles")
    tile = lax.axis_index("tiles")
    core = lax.axis_index("frames") % 2
    right_taper, upper_taper, lower_taper, exact, right_back, left_back, window = [jnp.asarray(t) for t in complex_tables()]
    numbers = jnp.stack([shifts[1, 0], shifts[0, 1], core, tile == tiles - 1, live_first[0], live_count[0]])
    numbers = jnp.broadcast_to(numbers.astype(jnp.int32)[:, None, None], (6, 8, side))

    to_left = [(i, i - 1) for i in range(1, tiles)]
    to_right = [(i, i + 1) for i in range(tiles - 1)]
    cores, halves = [[0, 1], [2, 3]], [[0, 2], [1, 3]]
    count_r = 8
    count_l = frames.shape[0] - count_r
    packed = [shape_of((n // 4, half, quad_width)) for n in (count_l, count_r)]
    own_l, own_r = call(pack_kernel, packed, 1)(frames)
    halo_l = lax.ppermute(own_l, "tiles", to_left)
    halo_r = lax.ppermute(own_r, "tiles", to_right)

    sums, folded = (4, 3, side, side), shape_of((2, folded_rows, side))
    spectrum = pltpu.VMEM((8, 2, side + half, side), float32)
    scratch = [pltpu.VMEM(sums, float32), pltpu.VMEM((2, 8, 2, side + half, side), float32)]
    tables = [shape_of(sums), shape_of((side, side))]
    tables += [shape_of((n // 4, 2 * side, 2 * width)) for n in (count_l, count_r)]
    before, inverse_eigen, rows_l, rows_r = call(start_kernel, tables, 6, [spectrum], 16 * 10**9)(
        numbers, own_l, own_r, right_taper, upper_taper, lower_taper
    )
    kept, sent = call(sum_kernel, [folded, folded], 6, scratch)(
        numbers, rows_r, halo_r, right_taper, upper_taper, inverse_eigen
    )
    both = lax.all_gather(sent, "frames", axis_index_groups=cores)
    (away,) = call(total_kernel, [folded], 3)(numbers, both, kept)
    back = lax.ppermute(away, "tiles", to_left)
    kept, sent = call(sum_kernel, [folded, folded], 7, scratch)(
        numbers, rows_l, halo_l, right_taper, lower_taper, away, before
    )
    both = lax.all_gather(sent, "frames", axis_index_groups=cores)
    (here,) = call(total_kernel, [folded], 4)(numbers, both, kept, back)
    both = lax.all_gather(here, "frames", axis_index_groups=halves)

    block = shape_of((half, width))
    upper, lower = call(solve_kernel, [block, shape_of((half, 2 * side))], 7)(
        numbers, both, exact, right_back, left_back, inverse_eigen, window
    )
    lower = lax.ppermute(lower, "tiles", to_right)
    (own,) = call(receive_kernel, [block], 3)(numbers, upper, lower)
    own = lax.all_gather(own, "frames", axis_index_groups=cores)
    return own[0] + own[1]


def solution(mesh):
    placed = (P("frames", "tiles", None), P("tiles"), P("tiles"), P())
    return jax.shard_map(on_device, mesh=mesh, in_specs=placed, out_specs=P("tiles", None), check_vma=False)
```

```python
import jax
import jax.numpy as jnp
import ml_dtypes
import numpy as np
from jax import lax
from jax.experimental import pallas as pl
from jax.experimental.pallas import tpu as pltpu
from jax.sharding import PartitionSpec as P

ridge_term = 0.1
share_term = 0.0001
tiny_term = 1e-06

side = 128
half = 64
width = 320
quad_width = 4 * width
folded_rows = 200
total_frames = 80
float32 = jnp.float32
bfloat16 = jnp.bfloat16
vmem_limit = 24 * 1024 * 1024


def as_pieces(table):
    upper = table.astype(np.float32).astype(ml_dtypes.bfloat16)
    lower = (table - upper.astype(np.float64)).astype(np.float32).astype(ml_dtypes.bfloat16)
    return upper, lower


def complex_tables():
    index = np.arange(side)
    angle = 2.0 * np.pi * (index[:, None] * index[None, :] % side) / side
    cosine, sine = np.cos(angle), np.sin(angle)
    taper = np.sin(np.pi * (index + 0.5) / side) ** 2
    wc, ws = taper[:, None] * cosine, taper[:, None] * sine
    right_taper = np.block([[wc, -ws], [ws, wc]])
    left_taper = np.block([[wc.T, ws.T], [-ws.T, wc.T]])
    right = np.block([[cosine, -sine], [sine, cosine]])
    left = np.block([[cosine, sine], [-sine, cosine]])
    right_back = np.block([[cosine, sine], [-sine, cosine]])
    left_back = np.block([[cosine, -sine], [sine, cosine]])
    window = (taper[:, None] * taper[None, :] / side**2).astype(np.float32)
    exact = np.stack([right, left, right_back, left_back]).astype(np.float32)
    rows = np.concatenate([index[:half], side + index[:half]])
    tapers = [deep(right_taper), wide(left_taper[:, rows]), wide(left_taper[:, rows + half])]
    return [*tapers, exact, deep(right_back), wide(left_back), window]


def deep(table):
    upper, lower = as_pieces(table)
    return np.concatenate([upper, upper, lower], axis=0)


def wide(table):
    upper, lower = as_pieces(table)
    return np.concatenate([upper, upper, lower], axis=1)


def pieces(values):
    upper = values.astype(bfloat16)
    lower = (values - upper.astype(float32)).astype(bfloat16)
    return upper, lower


def product(a, b):
    return jnp.dot(a, b, preferred_element_type=float32)


def times_table(values, table):
    upper, lower = pieces(values)
    return product(jnp.concatenate([upper, lower, upper], axis=1), table)


def table_times(table, values):
    upper, lower = pieces(values)
    return product(table, jnp.concatenate([upper, lower, upper], axis=0))


def exactly(a, b):
    return jnp.dot(a, b, precision=lax.Precision.HIGHEST, preferred_element_type=float32)


def upright(g):
    return jnp.concatenate([g[:, :side], g[:, side:]], axis=0)


def moved(values, row_step, col_step):
    return pltpu.roll(pltpu.roll(values, side - col_step, 1), side - row_step, 0)


def moved_back(values, row_step, col_step):
    return pltpu.roll(pltpu.roll(values, col_step, 1), row_step, 0)


def negation(step, twice_axis):
    down = lax.broadcasted_iota(jnp.int32, (side, side), 0)
    across = lax.broadcasted_iota(jnp.int32, (side, side), 1)
    once = jnp.where(((down + across + step) & (side - 1)) == 0, 1.0, 0.0).astype(bfloat16)
    return jnp.concatenate([once, once], axis=twice_axis)


def mirrored(planes, row_step, col_step, rows=side):
    upper, lower = pieces(jnp.concatenate(planes, axis=0))
    tall = product(jnp.concatenate([upper, lower], axis=1), negation(col_step, 0))
    across = jnp.concatenate([tall[i * side : (i + 1) * side] for i in range(len(planes))], axis=1)
    upper, lower = pieces(across)
    across = product(negation(row_step, 1)[:rows], jnp.concatenate([upper, lower], axis=0))
    return [across[:, i * side : (i + 1) * side] for i in range(len(planes))]


def pack_kernel(frames_ref, *out_refs):
    f = 0
    for out_ref in out_refs:
        for quad in range(out_ref.shape[0]):
            for j in range(2):
                one, two = frames_ref[f + j], frames_ref[f + 2 + j]
                base = 2 * width * j
                out_ref[quad, :, base : base + 256] = one[:, :256]
                out_ref[quad, :, base + 256 : base + 512] = two[:, :256]
                out_ref[quad, :, base + 512 : base + 640] = jnp.concatenate([one[:, 256:], two[:, 256:]], axis=1)
            f += 4


def rows_of(block, table):
    high, low = pieces(jnp.concatenate([block[:, : 2 * width], block[:, 2 * width :]], axis=0))
    return product(table, jnp.concatenate([high, low, high], axis=0))


def add_quad(g, row_step, col_step, right, spectrum, acc):
    places = []
    for piece in pieces(g):
        column = []
        for p in range(2):
            base = 256 * p
            last = 512 + half * p
            column.append(piece[:, base : base + 128])
            column.append(piece[:, base + half : base + half + 128])
            column.append(piece[:, base + 128 : base + 256])
            column.append(jnp.concatenate([piece[:, base + 192 : base + 256], piece[:, last : last + half]], axis=1))
        places.append(jnp.concatenate([jnp.concatenate([c[:side], c[side:]], axis=1) for c in column], axis=0))
    high, low = places
    z = product(jnp.concatenate([high, low, high], axis=1), right)
    for k in range(8):
        for part in range(2):
            plane = z[k * side : (k + 1) * side, part * side : (part + 1) * side]
            spectrum[k, part, 0:side] = plane
            spectrum[k, part, side : side + half] = plane[:half]
    for c in range(4):
        power, cross_a, cross_b = acc[c, 0], acc[c, 1], acc[c, 2]
        for k in (c, 4 + c):
            zr = z[k * side : (k + 1) * side, :side]
            zi = z[k * side : (k + 1) * side, side:]
            power = power + (zr * zr + zi * zi)
            yr = pltpu.roll(spectrum[k, 0, pl.ds(1, side)], side - col_step, 1)
            yi = pltpu.roll(spectrum[k, 1, pl.ds(1, side)], side - col_step, 1)
            cross_a = cross_a + (zi * yr - zr * yi)
            yr = pltpu.roll(spectrum[k, 0, pl.ds(row_step, side)], side - 1, 1)
            yi = pltpu.roll(spectrum[k, 1, pl.ds(row_step, side)], side - 1, 1)
            cross_b = cross_b + (zi * yr - zr * yi)
        acc[c, 0], acc[c, 1], acc[c, 2] = power, cross_a, cross_b


def number(numbers, i):
    return numbers[i][0, 0]


def fold(acc, row_step, col_step, lower_core, kept, sent):
    lanes = lax.broadcasted_iota(jnp.int32, (half, side), 1)
    top = folded_rows - side
    power = mirrored([acc[c, 0] for c in range(4)], 0, 0, 80)
    cross_a = mirrored([acc[c, 1] for c in range(4)], 1, col_step, half)
    cross_b = mirrored([acc[c, 2] for c in range(4)], row_step, 1)
    planes = []
    for c in range(4):
        total = acc[c, 2] + cross_b[c]
        total = jnp.where(lanes < half, total[:half], pltpu.roll(total[half:], half, 1))
        planes.append((acc[c, 1, :half] + cross_a[c], total, acc[c, 0, :top] + power[c][:top]))
    for j in range(2):
        for one, two, at in zip(planes[j], planes[2 + j], ((0, half), (half, side), (side, folded_rows))):
            kept[j, at[0] : at[1]] = jnp.where(lower_core, one, two)
            sent[j, at[0] : at[1]] = jnp.where(lower_core, two, one)


def start_kernel(
    numbers, own_l, own_r, right_ref, upper_ref, lower_ref, out_ref, eigen_ref, rows_l_ref, rows_r_ref, spectrum
):
    row_step, col_step = number(numbers, 0), number(numbers, 1)
    down = lax.broadcasted_iota(jnp.int32, (side, side), 0)
    across = lax.broadcasted_iota(jnp.int32, (side, side), 1)
    total = jnp.full((side, side), ridge_term, float32)
    for rows, cols in ((1, col_step), (row_step, 1)):
        angle = (down * rows + across * cols) & (side - 1)
        total = total + 2.0 - 2.0 * jnp.cos(angle.astype(float32) * (2.0 * np.pi / side))
    eigen_ref[...] = 1.0 / (total * (side * side))
    out_ref[...] = jnp.zeros_like(out_ref)
    for i in range(own_l.shape[0]):
        rows_l_ref[i] = rows_of(own_l[i], upper_ref[...])
    for i in range(own_r.shape[0]):
        rows_r_ref[i] = rows_of(own_r[i], lower_ref[...])

    @pl.when(number(numbers, 3) == 1)
    def last_tile():
        def body(i, carry):
            add_quad(rows_of(own_r[i], upper_ref[...]), row_step, col_step, right_ref[...], spectrum, out_ref)
            return carry

        lax.fori_loop(0, own_r.shape[0], body, 0)


def sum_kernel(numbers, own, halo, right_ref, left_ref, *refs):
    kept, sent, acc, spectrum = refs[-4:]
    row_step, col_step = number(numbers, 0), number(numbers, 1)
    acc[...] = refs[1][...] if len(refs) == 7 else jnp.zeros_like(acc)
    for i in range(halo.shape[0]):
        g = own[i] + rows_of(halo[i], left_ref[...])
        add_quad(g, row_step, col_step, right_ref[...], spectrum.at[i % 2], acc)
    fold(acc, row_step, col_step, number(numbers, 2) == 0, kept, sent)


def wave(angle):
    turns = jnp.floor(angle * (2.0 / np.pi) + 0.5)
    rest = angle - turns * np.float32(1.5703125)
    rest = rest - turns * np.float32(4.837512969970703125e-4)
    rest = rest - turns * np.float32(7.549789948768648e-8)
    square = rest * rest
    sine = rest + rest * square * (-1.6666654611e-1 + square * (8.3321608736e-3 - square * 1.9515295891e-4))
    cosine = 1.0 - 0.5 * square + square * square * (4.166664568298827e-2 + square * (-1.388731625493765e-3 + square * 2.443315711809948e-5))
    quarter = turns.astype(jnp.int32)
    odd = (quarter & 1) == 1
    first = jnp.where(odd, sine, cosine)
    second = jnp.where(odd, cosine, sine)
    first = jnp.where(((quarter + 1) & 2) == 2, -first, first)
    second = jnp.where((quarter & 2) == 2, -second, second)
    return first, second


def total_kernel(numbers, both, *refs):
    total = jnp.where(number(numbers, 2) == 0, both[1], both[0])
    for ref in refs[:-1]:
        total = total + ref[...]
    refs[-1][...] = total


def solve_kernel(numbers, halves, exact, right_back, left_back, inverse_eigen, window, upper_ref, lower_ref):
    row_step, col_step = number(numbers, 0), number(numbers, 1)
    live_first, live_last = number(numbers, 4), number(numbers, 4) + number(numbers, 5)
    lanes = lax.broadcasted_iota(jnp.int32, (side, side), 1)
    blank = jnp.zeros((half, side), float32)
    powers, crosses_a, crosses_b = [], [], []
    for j in range(2):
        both = halves[0, j] + halves[1, j]
        crowded = both[half:side]
        powers.append(jnp.concatenate([both[side:], blank[: 2 * side - folded_rows]], axis=0))
        crosses_a.append(jnp.concatenate([both[:half], blank], axis=0))
        spread = jnp.concatenate([crowded, pltpu.roll(crowded, half, 1)], axis=0)
        crosses_b.append(jnp.where(lanes < half, spread, 0.0))
    far_powers = mirrored(powers, 0, 0)
    far_a = mirrored(crosses_a, 1, col_step)
    far_b = mirrored(crosses_b, row_step, 1)
    scale = 0.5 / total_frames
    targets, amplitudes = [], []
    for j in range(2):
        power = jnp.concatenate([powers[j][: folded_rows - side], far_powers[j][folded_rows - side :]], axis=0)
        power = power * scale
        cross_a = (crosses_a[j] + far_a[j]) * scale
        cross_b = (crosses_b[j] + far_b[j]) * scale
        level = jnp.sum(jnp.sum(power, axis=0, keepdims=True), axis=1, keepdims=True) * (1.0 / (side * side))
        floor = share_term * level * level
        target = jnp.zeros((side, side), float32)
        for cross, rows, cols in ((cross_a, 1, col_step), (cross_b, row_step, 1)):
            partner = moved(power, rows, cols)
            coherence = cross / (jnp.sqrt(power * partner + floor) + tiny_term)
            target = target + coherence - moved_back(coherence, rows, cols)
        targets.append(target)
        amplitudes.append(jnp.sqrt(power))
    z = exactly(exact[1], upright(exactly(jnp.concatenate(targets, axis=1), exact[0])))
    zr = z[:side] * inverse_eigen[...]
    zi = z[side:] * inverse_eigen[...]
    phase = table_times(left_back[...], upright(times_table(jnp.concatenate([zr, zi], axis=1), right_back[...])))
    cosine, sine = wave(phase)
    first, second = amplitudes
    wr = first * cosine[:side] - second * sine[side:]
    wi = first * sine[:side] + second * cosine[side:]
    rebuilt = exactly(exact[3], upright(exactly(jnp.concatenate([wr, wi], axis=1), exact[2])))
    live = []
    for j in range(2):
        c = 2 * number(numbers, 2) + j
        live.append(jnp.where((c >= live_first) & (c < live_last), 1.0, 0.0).astype(float32))
    first = rebuilt[:side] * (window[...] * live[0])
    second = pltpu.roll(rebuilt[side:] * (window[...] * live[1]), half, 1)
    left_part = first + jnp.where(lanes >= half, second, 0.0)
    right_part = jnp.where(lanes < half, second, 0.0)
    for out_ref, at in ((upper_ref, 0), (lower_ref, half)):
        rest = right_part[at : at + half, :half]
        out_ref[:half] = left_part[at : at + half]
        out_ref[half:] = jnp.concatenate([rest[: half // 2], rest[half // 2 :]], axis=1)


def join_kernel(cores_ref, out_ref):
    lanes = lax.broadcasted_iota(jnp.int32, (half, side), 1)
    rests = []
    for core in range(2):
        rest = cores_ref[core, half:]
        rests.append(jnp.concatenate([rest, pltpu.roll(rest, half, 1)], axis=0))
    out_ref[:, 0:128] = cores_ref[0, :half]
    out_ref[:, 128:256] = cores_ref[1, :half] + jnp.where(lanes < half, rests[0], 0.0)
    out_ref[:, 256:320] = rests[1][:, :half]


vmem = pl.BlockSpec(memory_space=pltpu.VMEM)


def shape_of(dims, dtype=float32):
    return jax.ShapeDtypeStruct(dims, dtype)


def call(kernel, shapes, array_count, scratch=(), flops=0, moved_bytes=0):
    return pl.pallas_call(
        kernel,
        out_shape=shapes,
        in_specs=[vmem] * array_count,
        out_specs=[vmem] * len(shapes),
        scratch_shapes=list(scratch),
        compiler_params=pltpu.CompilerParams(vmem_limit_bytes=vmem_limit),
        cost_estimate=pl.CostEstimate(flops=flops, bytes_accessed=moved_bytes, transcendentals=0),
    )


def on_device(frames, live_first, live_count, shifts):
    tiles = lax.axis_size("tiles")
    tile = lax.axis_index("tiles")
    core = lax.axis_index("frames") % 2
    right_taper, upper_taper, lower_taper, exact, right_back, left_back, window = [jnp.asarray(t) for t in complex_tables()]
    numbers = jnp.stack([shifts[1, 0], shifts[0, 1], core, tile == tiles - 1, live_first[0], live_count[0]])
    numbers = jnp.broadcast_to(numbers.astype(jnp.int32)[:, None, None], (6, 8, side))

    to_left = [(i, i - 1) for i in range(1, tiles)]
    to_right = [(i, i + 1) for i in range(tiles - 1)]
    cores, halves = [[0, 1], [2, 3]], [[0, 2], [1, 3]]
    count_r = 8
    count_l = frames.shape[0] - count_r
    packed = [shape_of((n // 4, half, quad_width)) for n in (count_l, count_r)]
    own_l, own_r = call(pack_kernel, packed, 1)(frames)
    halo_l = lax.ppermute(own_l, "tiles", to_left)
    halo_r = lax.ppermute(own_r, "tiles", to_right)

    sums, folded = (4, 3, side, side), shape_of((2, folded_rows, side))
    spectrum = pltpu.VMEM((8, 2, side + half, side), float32)
    scratch = [pltpu.VMEM(sums, float32), pltpu.VMEM((2, 8, 2, side + half, side), float32)]
    tables = [shape_of(sums), shape_of((side, side))]
    tables += [shape_of((n // 4, 2 * side, 2 * width)) for n in (count_l, count_r)]
    before, inverse_eigen, rows_l, rows_r = call(start_kernel, tables, 6, [spectrum], 16 * 10**9)(
        numbers, own_l, own_r, right_taper, upper_taper, lower_taper
    )
    kept, sent = call(sum_kernel, [folded, folded], 6, scratch)(
        numbers, rows_r, halo_r, right_taper, upper_taper, own_r
    )
    both = lax.all_gather(sent, "frames", axis_index_groups=cores)
    (away,) = call(total_kernel, [folded], 3)(numbers, both, kept)
    back = lax.ppermute(away, "tiles", to_left)
    kept, sent = call(sum_kernel, [folded, folded], 8, scratch)(
        numbers, rows_l, halo_l, right_taper, lower_taper, away, before, own_l
    )
    both = lax.all_gather(sent, "frames", axis_index_groups=cores)
    (here,) = call(total_kernel, [folded], 4)(numbers, both, kept, back)
    both = lax.all_gather(here, "frames", axis_index_groups=halves)

    block = shape_of((half + half // 2, side))
    upper, lower = call(solve_kernel, [block, block], 7)(
        numbers, both, exact, right_back, left_back, inverse_eigen, window
    )
    own = upper + lax.ppermute(lower, "tiles", to_right)
    both = lax.all_gather(own, "frames", axis_index_groups=cores)
    (image,) = call(join_kernel, [shape_of((half, width))], 1)(both)
    return image


def solution(mesh):
    placed = (P("frames", "tiles", None), P("tiles"), P("tiles"), P())
    return jax.shard_map(on_device, mesh=mesh, in_specs=placed, out_specs=P("tiles", None), check_vma=False)
```

```python
import jax
import jax.numpy as jnp
import ml_dtypes
import numpy as np
from jax import lax
from jax.experimental import pallas as pl
from jax.experimental.pallas import tpu as pltpu
from jax.sharding import PartitionSpec as P

ridge_term = 0.1
share_term = 0.0001
tiny_term = 1e-06

side = 128
half = 64
width = 320
quad_width = 4 * width
folded_rows = 200
total_frames = 80
float32 = jnp.float32
bfloat16 = jnp.bfloat16
vmem_limit = 24 * 1024 * 1024


def as_pieces(table):
    upper = table.astype(np.float32).astype(ml_dtypes.bfloat16)
    lower = (table - upper.astype(np.float64)).astype(np.float32).astype(ml_dtypes.bfloat16)
    return upper, lower


def complex_tables():
    index = np.arange(side)
    angle = 2.0 * np.pi * (index[:, None] * index[None, :] % side) / side
    cosine, sine = np.cos(angle), np.sin(angle)
    taper = np.sin(np.pi * (index + 0.5) / side) ** 2
    wc, ws = taper[:, None] * cosine, taper[:, None] * sine
    right_taper = np.block([[wc, -ws], [ws, wc]])
    left_taper = np.block([[wc.T, ws.T], [-ws.T, wc.T]])
    right = np.block([[cosine, -sine], [sine, cosine]])
    left = np.block([[cosine, sine], [-sine, cosine]])
    right_back = np.block([[cosine, sine], [-sine, cosine]])
    left_back = np.block([[cosine, -sine], [sine, cosine]])
    window = (taper[:, None] * taper[None, :] / side**2).astype(np.float32)
    exact = np.stack([right, left, right_back, left_back]).astype(np.float32)
    rows = np.concatenate([index[:half], side + index[:half]])
    tapers = [deep(right_taper), wide(left_taper[:, rows]), wide(left_taper[:, rows + half])]
    return [*tapers, exact, deep(right_back), wide(left_back), window]


def deep(table):
    upper, lower = as_pieces(table)
    return np.concatenate([upper, upper, lower], axis=0)


def wide(table):
    upper, lower = as_pieces(table)
    return np.concatenate([upper, upper, lower], axis=1)


def pieces(values):
    upper = values.astype(bfloat16)
    lower = (values - upper.astype(float32)).astype(bfloat16)
    return upper, lower


def product(a, b):
    return jnp.dot(a, b, preferred_element_type=float32)


def times_table(values, table):
    upper, lower = pieces(values)
    return product(jnp.concatenate([upper, lower, upper], axis=1), table)


def table_times(table, values):
    upper, lower = pieces(values)
    return product(table, jnp.concatenate([upper, lower, upper], axis=0))


def exactly(a, b):
    return jnp.dot(a, b, precision=lax.Precision.HIGHEST, preferred_element_type=float32)


def upright(g):
    return jnp.concatenate([g[:, :side], g[:, side:]], axis=0)


def moved(values, row_step, col_step):
    return pltpu.roll(pltpu.roll(values, side - col_step, 1), side - row_step, 0)


def moved_back(values, row_step, col_step):
    return pltpu.roll(pltpu.roll(values, col_step, 1), row_step, 0)


def negation(step, twice_axis):
    down = lax.broadcasted_iota(jnp.int32, (side, side), 0)
    across = lax.broadcasted_iota(jnp.int32, (side, side), 1)
    once = jnp.where(((down + across + step) & (side - 1)) == 0, 1.0, 0.0).astype(bfloat16)
    return jnp.concatenate([once, once], axis=twice_axis)


def mirrored(planes, row_step, col_step, rows=side):
    upper, lower = pieces(jnp.concatenate(planes, axis=0))
    tall = product(jnp.concatenate([upper, lower], axis=1), negation(col_step, 0))
    across = jnp.concatenate([tall[i * side : (i + 1) * side] for i in range(len(planes))], axis=1)
    upper, lower = pieces(across)
    across = product(negation(row_step, 1)[:rows], jnp.concatenate([upper, lower], axis=0))
    return [across[:, i * side : (i + 1) * side] for i in range(len(planes))]


def pack_kernel(frames_ref, *out_refs):
    f = 0
    for out_ref in out_refs:
        for quad in range(out_ref.shape[0]):
            for j in range(2):
                one, two = frames_ref[f + j], frames_ref[f + 2 + j]
                base = 2 * width * j
                out_ref[quad, :, base : base + 256] = one[:, :256]
                out_ref[quad, :, base + 256 : base + 512] = two[:, :256]
                out_ref[quad, :, base + 512 : base + 640] = jnp.concatenate([one[:, 256:], two[:, 256:]], axis=1)
            f += 4


def rows_of(block, table):
    high, low = pieces(jnp.concatenate([block[:, : 2 * width], block[:, 2 * width :]], axis=0))
    return product(table, jnp.concatenate([high, low, high], axis=0))


def add_quad(g, row_step, col_step, right, spectrum, acc):
    places = []
    for piece in pieces(g):
        column = []
        for p in range(2):
            base = 256 * p
            last = 512 + half * p
            column.append(piece[:, base : base + 128])
            column.append(piece[:, base + half : base + half + 128])
            column.append(piece[:, base + 128 : base + 256])
            column.append(jnp.concatenate([piece[:, base + 192 : base + 256], piece[:, last : last + half]], axis=1))
        places.append(jnp.concatenate([jnp.concatenate([c[:side], c[side:]], axis=1) for c in column], axis=0))
    high, low = places
    z = product(jnp.concatenate([high, low, high], axis=1), right)
    for k in range(8):
        for part in range(2):
            plane = z[k * side : (k + 1) * side, part * side : (part + 1) * side]
            spectrum[k, part, 0:side] = plane
            spectrum[k, part, side : side + half] = plane[:half]
    for c in range(4):
        power, cross_a, cross_b = acc[c, 0], acc[c, 1], acc[c, 2]
        for k in (c, 4 + c):
            zr = z[k * side : (k + 1) * side, :side]
            zi = z[k * side : (k + 1) * side, side:]
            power = power + (zr * zr + zi * zi)
            yr = pltpu.roll(spectrum[k, 0, pl.ds(1, side)], side - col_step, 1)
            yi = pltpu.roll(spectrum[k, 1, pl.ds(1, side)], side - col_step, 1)
            cross_a = cross_a + (zi * yr - zr * yi)
            yr = pltpu.roll(spectrum[k, 0, pl.ds(row_step, side)], side - 1, 1)
            yi = pltpu.roll(spectrum[k, 1, pl.ds(row_step, side)], side - 1, 1)
            cross_b = cross_b + (zi * yr - zr * yi)
        acc[c, 0], acc[c, 1], acc[c, 2] = power, cross_a, cross_b


def number(numbers, i):
    return numbers[i][0, 0]


def fold(acc, row_step, col_step, lower_core, kept, sent):
    lanes = lax.broadcasted_iota(jnp.int32, (half, side), 1)
    top = folded_rows - side
    power = mirrored([acc[c, 0] for c in range(4)], 0, 0, 80)
    cross_a = mirrored([acc[c, 1] for c in range(4)], 1, col_step, half)
    cross_b = mirrored([acc[c, 2] for c in range(4)], row_step, 1)
    planes = []
    for c in range(4):
        total = acc[c, 2] + cross_b[c]
        total = jnp.where(lanes < half, total[:half], pltpu.roll(total[half:], half, 1))
        planes.append((acc[c, 1, :half] + cross_a[c], total, acc[c, 0, :top] + power[c][:top]))
    for j in range(2):
        for one, two, at in zip(planes[j], planes[2 + j], ((0, half), (half, side), (side, folded_rows))):
            kept[j, at[0] : at[1]] = jnp.where(lower_core, one, two)
            sent[j, at[0] : at[1]] = jnp.where(lower_core, two, one)


def start_kernel(
    numbers, own_l, own_r, right_ref, upper_ref, lower_ref, out_ref, eigen_ref, rows_l_ref, rows_r_ref, spectrum
):
    row_step, col_step = number(numbers, 0), number(numbers, 1)
    down = lax.broadcasted_iota(jnp.int32, (side, side), 0)
    across = lax.broadcasted_iota(jnp.int32, (side, side), 1)
    total = jnp.full((side, side), ridge_term, float32)
    for rows, cols in ((1, col_step), (row_step, 1)):
        angle = (down * rows + across * cols) & (side - 1)
        total = total + 2.0 - 2.0 * jnp.cos(angle.astype(float32) * (2.0 * np.pi / side))
    eigen_ref[...] = 1.0 / (total * (side * side))
    out_ref[...] = jnp.zeros_like(out_ref)
    for i in range(own_l.shape[0]):
        rows_l_ref[i] = rows_of(own_l[i], upper_ref[...])
    for i in range(own_r.shape[0]):
        rows_r_ref[i] = rows_of(own_r[i], lower_ref[...])

    @pl.when(number(numbers, 3) == 1)
    def last_tile():
        def body(i, carry):
            add_quad(rows_of(own_r[i], upper_ref[...]), row_step, col_step, right_ref[...], spectrum, out_ref)
            return carry

        lax.fori_loop(0, own_r.shape[0], body, 0)


def sum_kernel(numbers, own, halo, right_ref, left_ref, *refs):
    kept, sent, acc, spectrum = refs[-4:]
    row_step, col_step = number(numbers, 0), number(numbers, 1)
    acc[...] = refs[1][...] if len(refs) == 7 else jnp.zeros_like(acc)
    for i in range(halo.shape[0]):
        g = own[i] + rows_of(halo[i], left_ref[...])
        add_quad(g, row_step, col_step, right_ref[...], spectrum.at[i % 2], acc)
    fold(acc, row_step, col_step, number(numbers, 2) == 0, kept, sent)


def wave(angle):
    turns = jnp.floor(angle * (2.0 / np.pi) + 0.5)
    rest = angle - turns * np.float32(1.5703125)
    rest = rest - turns * np.float32(4.837512969970703125e-4)
    rest = rest - turns * np.float32(7.549789948768648e-8)
    square = rest * rest
    sine = rest + rest * square * (-1.6666654611e-1 + square * (8.3321608736e-3 - square * 1.9515295891e-4))
    cosine = 1.0 - 0.5 * square + square * square * (4.166664568298827e-2 + square * (-1.388731625493765e-3 + square * 2.443315711809948e-5))
    quarter = turns.astype(jnp.int32)
    odd = (quarter & 1) == 1
    first = jnp.where(odd, sine, cosine)
    second = jnp.where(odd, cosine, sine)
    first = jnp.where(((quarter + 1) & 2) == 2, -first, first)
    second = jnp.where((quarter & 2) == 2, -second, second)
    return first, second


def total_kernel(numbers, both, *refs):
    total = jnp.where(number(numbers, 2) == 0, both[1], both[0])
    for ref in refs[:-1]:
        total = total + ref[...]
    refs[-1][...] = total


def solve_kernel(numbers, halves, exact, right_back, left_back, inverse_eigen, window, upper_ref, lower_ref):
    row_step, col_step = number(numbers, 0), number(numbers, 1)
    live_first, live_last = number(numbers, 4), number(numbers, 4) + number(numbers, 5)
    lanes = lax.broadcasted_iota(jnp.int32, (side, side), 1)
    blank = jnp.zeros((half, side), float32)
    powers, crosses_a, crosses_b = [], [], []
    for j in range(2):
        both = halves[0, j] + halves[1, j]
        crowded = both[half:side]
        powers.append(jnp.concatenate([both[side:], blank[: 2 * side - folded_rows]], axis=0))
        crosses_a.append(jnp.concatenate([both[:half], blank], axis=0))
        spread = jnp.concatenate([crowded, pltpu.roll(crowded, half, 1)], axis=0)
        crosses_b.append(jnp.where(lanes < half, spread, 0.0))
    far_powers = mirrored(powers, 0, 0)
    far_a = mirrored(crosses_a, 1, col_step)
    far_b = mirrored(crosses_b, row_step, 1)
    scale = 0.5 / total_frames
    targets, amplitudes = [], []
    for j in range(2):
        power = jnp.concatenate([powers[j][: folded_rows - side], far_powers[j][folded_rows - side :]], axis=0)
        power = power * scale
        cross_a = (crosses_a[j] + far_a[j]) * scale
        cross_b = (crosses_b[j] + far_b[j]) * scale
        level = jnp.sum(jnp.sum(power, axis=0, keepdims=True), axis=1, keepdims=True) * (1.0 / (side * side))
        floor = share_term * level * level
        target = jnp.zeros((side, side), float32)
        for cross, rows, cols in ((cross_a, 1, col_step), (cross_b, row_step, 1)):
            partner = moved(power, rows, cols)
            coherence = cross / (jnp.sqrt(power * partner + floor) + tiny_term)
            target = target + coherence - moved_back(coherence, rows, cols)
        targets.append(target)
        amplitudes.append(jnp.sqrt(power))
    z = exactly(exact[1], upright(exactly(jnp.concatenate(targets, axis=1), exact[0])))
    zr = z[:side] * inverse_eigen[...]
    zi = z[side:] * inverse_eigen[...]
    phase = table_times(left_back[...], upright(times_table(jnp.concatenate([zr, zi], axis=1), right_back[...])))
    cosine, sine = wave(phase)
    first, second = amplitudes
    wr = first * cosine[:side] - second * sine[side:]
    wi = first * sine[:side] + second * cosine[side:]
    rebuilt = exactly(exact[3], upright(exactly(jnp.concatenate([wr, wi], axis=1), exact[2])))
    live = []
    for j in range(2):
        c = 2 * number(numbers, 2) + j
        live.append(jnp.where((c >= live_first) & (c < live_last), 1.0, 0.0).astype(float32))
    first = rebuilt[:side] * (window[...] * live[0])
    second = pltpu.roll(rebuilt[side:] * (window[...] * live[1]), half, 1)
    left_part = first + jnp.where(lanes >= half, second, 0.0)
    right_part = jnp.where(lanes < half, second, 0.0)
    for out_ref, at in ((upper_ref, 0), (lower_ref, half)):
        rest = right_part[at : at + half, :half]
        out_ref[:half] = left_part[at : at + half]
        out_ref[half:] = jnp.concatenate([rest[: half // 2], rest[half // 2 :]], axis=1)


def join_kernel(uppers, lowers, out_ref):
    lanes = lax.broadcasted_iota(jnp.int32, (half, side), 1)
    firsts, rests = [], []
    for core in range(2):
        block = uppers[core] + lowers[core]
        rest = block[half:]
        firsts.append(block[:half])
        rests.append(jnp.concatenate([rest, pltpu.roll(rest, half, 1)], axis=0))
    out_ref[:, 0:128] = firsts[0]
    out_ref[:, 128:256] = firsts[1] + jnp.where(lanes < half, rests[0], 0.0)
    out_ref[:, 256:320] = rests[1][:, :half]


vmem = pl.BlockSpec(memory_space=pltpu.VMEM)


def shape_of(dims, dtype=float32):
    return jax.ShapeDtypeStruct(dims, dtype)


def call(kernel, shapes, array_count, scratch=(), flops=0, moved_bytes=0):
    return pl.pallas_call(
        kernel,
        out_shape=shapes,
        in_specs=[vmem] * array_count,
        out_specs=[vmem] * len(shapes),
        scratch_shapes=list(scratch),
        compiler_params=pltpu.CompilerParams(vmem_limit_bytes=vmem_limit),
        cost_estimate=pl.CostEstimate(flops=flops, bytes_accessed=moved_bytes, transcendentals=0),
    )


def on_device(frames, live_first, live_count, shifts):
    tiles = lax.axis_size("tiles")
    tile = lax.axis_index("tiles")
    core = lax.axis_index("frames") % 2
    right_taper, upper_taper, lower_taper, exact, right_back, left_back, window = [jnp.asarray(t) for t in complex_tables()]
    numbers = jnp.stack([shifts[1, 0], shifts[0, 1], core, tile == tiles - 1, live_first[0], live_count[0]])
    numbers = jnp.broadcast_to(numbers.astype(jnp.int32)[:, None, None], (6, 8, side))

    to_left = [(i, i - 1) for i in range(1, tiles)]
    to_right = [(i, i + 1) for i in range(tiles - 1)]
    cores, halves = [[0, 1], [2, 3]], [[0, 2], [1, 3]]
    count_r = 8
    count_l = frames.shape[0] - count_r
    packed = [shape_of((n // 4, half, quad_width)) for n in (count_l, count_r)]
    own_l, own_r = call(pack_kernel, packed, 1)(frames)
    halo_l = lax.ppermute(own_l, "tiles", to_left)
    halo_r = lax.ppermute(own_r, "tiles", to_right)

    sums, folded = (4, 3, side, side), shape_of((2, folded_rows, side))
    spectrum = pltpu.VMEM((8, 2, side + half, side), float32)
    scratch = [pltpu.VMEM(sums, float32), pltpu.VMEM((2, 8, 2, side + half, side), float32)]
    tables = [shape_of(sums), shape_of((side, side))]
    tables += [shape_of((n // 4, 2 * side, 2 * width)) for n in (count_l, count_r)]
    before, inverse_eigen, rows_l, rows_r = call(start_kernel, tables, 6, [spectrum], 16 * 10**9)(
        numbers, own_l, own_r, right_taper, upper_taper, lower_taper
    )
    kept, sent = call(sum_kernel, [folded, folded], 6, scratch)(
        numbers, rows_r, halo_r, right_taper, upper_taper, own_r
    )
    both = lax.all_gather(sent, "frames", axis_index_groups=cores)
    (away,) = call(total_kernel, [folded], 3)(numbers, both, kept)
    back = lax.ppermute(away, "tiles", to_left)
    kept, sent = call(sum_kernel, [folded, folded], 8, scratch)(
        numbers, rows_l, halo_l, right_taper, lower_taper, away, before, own_l
    )
    both = lax.all_gather(sent, "frames", axis_index_groups=cores)
    (here,) = call(total_kernel, [folded], 4)(numbers, both, kept, back)
    both = lax.all_gather(here, "frames", axis_index_groups=halves)

    block = shape_of((half + half // 2, side))
    upper, lower = call(solve_kernel, [block, block], 7)(
        numbers, both, exact, right_back, left_back, inverse_eigen, window
    )
    lower = lax.ppermute(lower, "tiles", to_right)
    uppers = lax.all_gather(upper, "frames", axis_index_groups=cores)
    lowers = lax.all_gather(lower, "frames", axis_index_groups=cores)
    (image,) = call(join_kernel, [shape_of((half, width))], 2)(uppers, lowers)
    return image


def solution(mesh):
    placed = (P("frames", "tiles", None), P("tiles"), P("tiles"), P())
    return jax.shard_map(on_device, mesh=mesh, in_specs=placed, out_specs=P("tiles", None), check_vma=False)
```

```python
import jax
import jax.numpy as jnp
import ml_dtypes
import numpy as np
from jax import lax
from jax.experimental import pallas as pl
from jax.experimental.pallas import tpu as pltpu
from jax.sharding import PartitionSpec as P

ridge_term = 0.1
share_term = 0.0001
tiny_term = 1e-06

side = 128
half = 64
width = 320
quad_width = 4 * width
folded_rows = 200
total_frames = 80
float32 = jnp.float32
bfloat16 = jnp.bfloat16
vmem_limit = 24 * 1024 * 1024


def as_pieces(table):
    upper = table.astype(np.float32).astype(ml_dtypes.bfloat16)
    lower = (table - upper.astype(np.float64)).astype(np.float32).astype(ml_dtypes.bfloat16)
    return upper, lower


def complex_tables():
    index = np.arange(side)
    angle = 2.0 * np.pi * (index[:, None] * index[None, :] % side) / side
    cosine, sine = np.cos(angle), np.sin(angle)
    taper = np.sin(np.pi * (index + 0.5) / side) ** 2
    wc, ws = taper[:, None] * cosine, taper[:, None] * sine
    right_taper = np.block([[wc, -ws], [ws, wc]])
    left_taper = np.block([[wc.T, ws.T], [-ws.T, wc.T]])
    right = np.block([[cosine, -sine], [sine, cosine]])
    left = np.block([[cosine, sine], [-sine, cosine]])
    right_back = np.block([[cosine, sine], [-sine, cosine]])
    left_back = np.block([[cosine, -sine], [sine, cosine]])
    window = (taper[:, None] * taper[None, :] / side**2).astype(np.float32)
    exact = np.stack([right, left, right_back, left_back]).astype(np.float32)
    rows = np.concatenate([index[:half], side + index[:half]])
    tapers = [deep(right_taper), wide(left_taper[:, rows]), wide(left_taper[:, rows + half])]
    return [*tapers, exact, deep(right_back), wide(left_back), window]


def deep(table):
    upper, lower = as_pieces(table)
    return np.concatenate([upper, upper, lower], axis=0)


def wide(table):
    upper, lower = as_pieces(table)
    return np.concatenate([upper, upper, lower], axis=1)


def pieces(values):
    upper = values.astype(bfloat16)
    lower = (values - upper.astype(float32)).astype(bfloat16)
    return upper, lower


def product(a, b):
    return jnp.dot(a, b, preferred_element_type=float32)


def times_table(values, table):
    upper, lower = pieces(values)
    return product(jnp.concatenate([upper, lower, upper], axis=1), table)


def table_times(table, values):
    upper, lower = pieces(values)
    return product(table, jnp.concatenate([upper, lower, upper], axis=0))


def exactly(a, b):
    return jnp.dot(a, b, precision=lax.Precision.HIGHEST, preferred_element_type=float32)


def upright(g):
    return jnp.concatenate([g[:, :side], g[:, side:]], axis=0)


def moved(values, row_step, col_step):
    return pltpu.roll(pltpu.roll(values, side - col_step, 1), side - row_step, 0)


def moved_back(values, row_step, col_step):
    return pltpu.roll(pltpu.roll(values, col_step, 1), row_step, 0)


def negation(step, twice_axis):
    down = lax.broadcasted_iota(jnp.int32, (side, side), 0)
    across = lax.broadcasted_iota(jnp.int32, (side, side), 1)
    once = jnp.where(((down + across + step) & (side - 1)) == 0, 1.0, 0.0).astype(bfloat16)
    return jnp.concatenate([once, once], axis=twice_axis)


def mirrored(planes, row_step, col_step, rows=side):
    upper, lower = pieces(jnp.concatenate(planes, axis=0))
    tall = product(jnp.concatenate([upper, lower], axis=1), negation(col_step, 0))
    across = jnp.concatenate([tall[i * side : (i + 1) * side] for i in range(len(planes))], axis=1)
    upper, lower = pieces(across)
    across = product(negation(row_step, 1)[:rows], jnp.concatenate([upper, lower], axis=0))
    return [across[:, i * side : (i + 1) * side] for i in range(len(planes))]


def pack_kernel(frames_ref, *out_refs):
    f = 0
    for out_ref in out_refs:
        for quad in range(out_ref.shape[0]):
            for j in range(2):
                one, two = frames_ref[f + j], frames_ref[f + 2 + j]
                base = 2 * width * j
                out_ref[quad, :, base : base + 256] = one[:, :256]
                out_ref[quad, :, base + 256 : base + 512] = two[:, :256]
                out_ref[quad, :, base + 512 : base + 640] = jnp.concatenate([one[:, 256:], two[:, 256:]], axis=1)
            f += 4


def rows_of(block, table):
    high, low = pieces(jnp.concatenate([block[:, : 2 * width], block[:, 2 * width :]], axis=0))
    return product(table, jnp.concatenate([high, low, high], axis=0))


def add_quad(g, row_step, col_step, right, spectrum, acc):
    places = []
    for piece in pieces(g):
        column = []
        for p in range(2):
            base = 256 * p
            last = 512 + half * p
            column.append(piece[:, base : base + 128])
            column.append(piece[:, base + half : base + half + 128])
            column.append(piece[:, base + 128 : base + 256])
            column.append(jnp.concatenate([piece[:, base + 192 : base + 256], piece[:, last : last + half]], axis=1))
        places.append(jnp.concatenate([jnp.concatenate([c[:side], c[side:]], axis=1) for c in column], axis=0))
    high, low = places
    z = product(jnp.concatenate([high, low, high], axis=1), right)
    for k in range(8):
        for part in range(2):
            plane = z[k * side : (k + 1) * side, part * side : (part + 1) * side]
            spectrum[k, part, 0:side] = plane
            spectrum[k, part, side : side + half] = plane[:half]
    for c in range(4):
        power, cross_a, cross_b = acc[c, 0], acc[c, 1], acc[c, 2]
        for k in (c, 4 + c):
            zr = z[k * side : (k + 1) * side, :side]
            zi = z[k * side : (k + 1) * side, side:]
            power = power + (zr * zr + zi * zi)
            yr = pltpu.roll(spectrum[k, 0, pl.ds(1, side)], side - col_step, 1)
            yi = pltpu.roll(spectrum[k, 1, pl.ds(1, side)], side - col_step, 1)
            cross_a = cross_a + (zi * yr - zr * yi)
            yr = pltpu.roll(spectrum[k, 0, pl.ds(row_step, side)], side - 1, 1)
            yi = pltpu.roll(spectrum[k, 1, pl.ds(row_step, side)], side - 1, 1)
            cross_b = cross_b + (zi * yr - zr * yi)
        acc[c, 0], acc[c, 1], acc[c, 2] = power, cross_a, cross_b


def number(numbers, i):
    return numbers[i][0, 0]


def fold(acc, row_step, col_step, lower_core, kept, sent):
    lanes = lax.broadcasted_iota(jnp.int32, (half, side), 1)
    top = folded_rows - side
    power = mirrored([acc[c, 0] for c in range(4)], 0, 0, 80)
    cross_a = mirrored([acc[c, 1] for c in range(4)], 1, col_step, half)
    cross_b = mirrored([acc[c, 2] for c in range(4)], row_step, 1)
    planes = []
    for c in range(4):
        total = acc[c, 2] + cross_b[c]
        total = jnp.where(lanes < half, total[:half], pltpu.roll(total[half:], half, 1))
        planes.append((acc[c, 1, :half] + cross_a[c], total, acc[c, 0, :top] + power[c][:top]))
    for j in range(2):
        for one, two, at in zip(planes[j], planes[2 + j], ((0, half), (half, side), (side, folded_rows))):
            kept[j, at[0] : at[1]] = jnp.where(lower_core, one, two)
            sent[j, at[0] : at[1]] = jnp.where(lower_core, two, one)


def start_kernel(
    numbers, own_l, own_r, right_ref, upper_ref, lower_ref, out_ref, eigen_ref, rows_l_ref, rows_r_ref, spectrum
):
    row_step, col_step = number(numbers, 0), number(numbers, 1)
    down = lax.broadcasted_iota(jnp.int32, (side, side), 0)
    across = lax.broadcasted_iota(jnp.int32, (side, side), 1)
    total = jnp.full((side, side), ridge_term, float32)
    for rows, cols in ((1, col_step), (row_step, 1)):
        angle = (down * rows + across * cols) & (side - 1)
        total = total + 2.0 - 2.0 * jnp.cos(angle.astype(float32) * (2.0 * np.pi / side))
    eigen_ref[...] = 1.0 / (total * (side * side))
    out_ref[...] = jnp.zeros_like(out_ref)
    for i in range(own_l.shape[0]):
        rows_l_ref[i] = rows_of(own_l[i], upper_ref[...])
    for i in range(own_r.shape[0]):
        rows_r_ref[i] = rows_of(own_r[i], lower_ref[...])

    @pl.when(number(numbers, 3) == 1)
    def last_tile():
        def body(i, carry):
            add_quad(rows_of(own_r[i], upper_ref[...]), row_step, col_step, right_ref[...], spectrum, out_ref)
            return carry

        lax.fori_loop(0, own_r.shape[0], body, 0)


def sum_kernel(numbers, own, halo, right_ref, left_ref, *refs):
    kept, sent, acc, spectrum = refs[-4:]
    row_step, col_step = number(numbers, 0), number(numbers, 1)
    acc[...] = refs[1][...] if len(refs) == 7 else jnp.zeros_like(acc)
    for i in range(halo.shape[0]):
        g = own[i] + rows_of(halo[i], left_ref[...])
        add_quad(g, row_step, col_step, right_ref[...], spectrum.at[i % 2], acc)
    fold(acc, row_step, col_step, number(numbers, 2) == 0, kept, sent)


def wave(angle):
    turns = jnp.floor(angle * (2.0 / np.pi) + 0.5)
    rest = angle - turns * np.float32(1.5703125)
    rest = rest - turns * np.float32(4.837512969970703125e-4)
    rest = rest - turns * np.float32(7.549789948768648e-8)
    square = rest * rest
    sine = rest + rest * square * (-1.6666654611e-1 + square * (8.3321608736e-3 - square * 1.9515295891e-4))
    cosine = 1.0 - 0.5 * square + square * square * (4.166664568298827e-2 + square * (-1.388731625493765e-3 + square * 2.443315711809948e-5))
    quarter = turns.astype(jnp.int32)
    odd = (quarter & 1) == 1
    first = jnp.where(odd, sine, cosine)
    second = jnp.where(odd, cosine, sine)
    first = jnp.where(((quarter + 1) & 2) == 2, -first, first)
    second = jnp.where((quarter & 2) == 2, -second, second)
    return first, second


def total_kernel(numbers, both, *refs):
    total = jnp.where(number(numbers, 2) == 0, both[1], both[0])
    for ref in refs[:-1]:
        total = total + ref[...]
    refs[-1][...] = total


def solve_kernel(numbers, halves, exact, right_back, left_back, inverse_eigen, window, upper_ref, lower_ref):
    row_step, col_step = number(numbers, 0), number(numbers, 1)
    live_first, live_last = number(numbers, 4), number(numbers, 4) + number(numbers, 5)
    lanes = lax.broadcasted_iota(jnp.int32, (side, side), 1)
    blank = jnp.zeros((half, side), float32)
    powers, crosses_a, crosses_b = [], [], []
    for j in range(2):
        both = halves[0, j] + halves[1, j]
        crowded = both[half:side]
        powers.append(jnp.concatenate([both[side:], blank[: 2 * side - folded_rows]], axis=0))
        crosses_a.append(jnp.concatenate([both[:half], blank], axis=0))
        spread = jnp.concatenate([crowded, pltpu.roll(crowded, half, 1)], axis=0)
        crosses_b.append(jnp.where(lanes < half, spread, 0.0))
    far_powers = mirrored(powers, 0, 0)
    far_a = mirrored(crosses_a, 1, col_step)
    far_b = mirrored(crosses_b, row_step, 1)
    scale = 0.5 / total_frames
    targets, amplitudes = [], []
    for j in range(2):
        power = jnp.concatenate([powers[j][: folded_rows - side], far_powers[j][folded_rows - side :]], axis=0)
        power = power * scale
        cross_a = (crosses_a[j] + far_a[j]) * scale
        cross_b = (crosses_b[j] + far_b[j]) * scale
        level = jnp.sum(jnp.sum(power, axis=0, keepdims=True), axis=1, keepdims=True) * (1.0 / (side * side))
        floor = share_term * level * level
        target = jnp.zeros((side, side), float32)
        for cross, rows, cols in ((cross_a, 1, col_step), (cross_b, row_step, 1)):
            partner = moved(power, rows, cols)
            coherence = cross / (jnp.sqrt(power * partner + floor) + tiny_term)
            target = target + coherence - moved_back(coherence, rows, cols)
        targets.append(target)
        amplitudes.append(jnp.sqrt(power))
    z = exactly(exact[1], upright(exactly(jnp.concatenate(targets, axis=1), exact[0])))
    zr = z[:side] * inverse_eigen[...]
    zi = z[side:] * inverse_eigen[...]
    phase = table_times(left_back[...], upright(times_table(jnp.concatenate([zr, zi], axis=1), right_back[...])))
    cosine, sine = wave(phase)
    first, second = amplitudes
    wr = first * cosine[:side] - second * sine[side:]
    wi = first * sine[:side] + second * cosine[side:]
    rebuilt = exactly(exact[3], upright(exactly(jnp.concatenate([wr, wi], axis=1), exact[2])))
    live = []
    for j in range(2):
        c = 2 * number(numbers, 2) + j
        live.append(jnp.where((c >= live_first) & (c < live_last), 1.0, 0.0).astype(float32))
    first = rebuilt[:side] * (window[...] * live[0])
    second = pltpu.roll(rebuilt[side:] * (window[...] * live[1]), half, 1)
    left_part = first + jnp.where(lanes >= half, second, 0.0)
    right_part = jnp.where(lanes < half, second, 0.0)
    for out_ref, at in ((upper_ref, 0), (lower_ref, half)):
        rest = right_part[at : at + half, :half]
        out_ref[:half] = left_part[at : at + half]
        out_ref[half:] = jnp.concatenate([rest[: half // 2], rest[half // 2 :]], axis=1)


def join_kernel(cores_ref, out_ref):
    lanes = lax.broadcasted_iota(jnp.int32, (half, side), 1)
    rests = []
    for core in range(2):
        rest = cores_ref[core, half:]
        rests.append(jnp.concatenate([rest, pltpu.roll(rest, half, 1)], axis=0))
    out_ref[:, 0:128] = cores_ref[0, :half]
    out_ref[:, 128:256] = cores_ref[1, :half] + jnp.where(lanes < half, rests[0], 0.0)
    out_ref[:, 256:320] = rests[1][:, :half]


vmem = pl.BlockSpec(memory_space=pltpu.VMEM)


def shape_of(dims, dtype=float32):
    return jax.ShapeDtypeStruct(dims, dtype)


def call(kernel, shapes, array_count, scratch=(), flops=0, moved_bytes=0):
    return pl.pallas_call(
        kernel,
        out_shape=shapes,
        in_specs=[vmem] * array_count,
        out_specs=[vmem] * len(shapes),
        scratch_shapes=list(scratch),
        compiler_params=pltpu.CompilerParams(vmem_limit_bytes=vmem_limit),
        cost_estimate=pl.CostEstimate(flops=flops, bytes_accessed=moved_bytes, transcendentals=0),
    )


def on_device(frames, live_first, live_count, shifts):
    tiles = lax.axis_size("tiles")
    tile = lax.axis_index("tiles")
    core = lax.axis_index("frames") % 2
    right_taper, upper_taper, lower_taper, exact, right_back, left_back, window = [jnp.asarray(t) for t in complex_tables()]
    numbers = jnp.stack([shifts[1, 0], shifts[0, 1], core, tile == tiles - 1, live_first[0], live_count[0]])
    numbers = jnp.broadcast_to(numbers.astype(jnp.int32)[:, None, None], (6, 8, side))

    to_left = [(i, i - 1) for i in range(1, tiles)]
    to_right = [(i, i + 1) for i in range(tiles - 1)]
    cores, halves = [[0, 1], [2, 3]], [[0, 2], [1, 3]]
    layer = 16
    places = [(g, i, g ^ 2 if i % layer == layer - 1 else g, i + 1) for g in range(4) for i in range(tiles - 1)]
    sums_left = [(h * tiles + j, g * tiles + i) for g, i, h, j in places]
    count_r = 8
    count_l = frames.shape[0] - count_r
    packed = [shape_of((n // 4, half, quad_width)) for n in (count_l, count_r)]
    own_l, own_r = call(pack_kernel, packed, 1)(frames)
    halo_l = lax.ppermute(own_l, "tiles", to_left)
    halo_r = lax.ppermute(own_r, "tiles", to_right)

    sums, folded = (4, 3, side, side), shape_of((2, folded_rows, side))
    spectrum = pltpu.VMEM((8, 2, side + half, side), float32)
    scratch = [pltpu.VMEM(sums, float32), pltpu.VMEM((2, 8, 2, side + half, side), float32)]
    tables = [shape_of(sums), shape_of((side, side))]
    tables += [shape_of((n // 4, 2 * side, 2 * width)) for n in (count_l, count_r)]
    before, inverse_eigen, rows_l, rows_r = call(start_kernel, tables, 6, [spectrum], 16 * 10**9)(
        numbers, own_l, own_r, right_taper, upper_taper, lower_taper
    )
    kept, sent = call(sum_kernel, [folded, folded], 6, scratch)(
        numbers, rows_r, halo_r, right_taper, upper_taper, own_r
    )
    both = lax.all_gather(sent, "frames", axis_index_groups=cores)
    (away,) = call(total_kernel, [folded], 3)(numbers, both, kept)
    back = lax.ppermute(away, ("frames", "tiles"), sums_left)
    kept, sent = call(sum_kernel, [folded, folded], 8, scratch)(
        numbers, rows_l, halo_l, right_taper, lower_taper, away, before, own_l
    )
    both = lax.all_gather(sent, "frames", axis_index_groups=cores)
    (here,) = call(total_kernel, [folded], 4)(numbers, both, kept, back)
    both = lax.all_gather(here, "frames", axis_index_groups=halves)

    block = shape_of((half + half // 2, side))
    upper, lower = call(solve_kernel, [block, block], 7)(
        numbers, both, exact, right_back, left_back, inverse_eigen, window
    )
    own = upper + lax.ppermute(lower, "tiles", to_right)
    both = lax.all_gather(own, "frames", axis_index_groups=cores)
    (image,) = call(join_kernel, [shape_of((half, width))], 1)(both)
    return image


def solution(mesh):
    placed = (P("frames", "tiles", None), P("tiles"), P("tiles"), P())
    return jax.shard_map(on_device, mesh=mesh, in_specs=placed, out_specs=P("tiles", None), check_vma=False)
```
